512 devices in a mesh: lat: 8 (over x_lo, y), lon: 64 (over x_hi, z, core).
Axes of the slice: x: 4 (x_hi: 2, x_lo: 2; x = x_hi * 2 + x_lo), y: 4, z: 16, core: 2. Of those that a mesh axis runs over, the one named last changes fastest.
Arguments:
- input_field: float32 [96, 128, 8192], P(None, 'lat', 'lon'), may hold values from -6 to 6
- conv_weight: float32 [96, 864], replicated, may hold values from -0.21875 to 0.21875
- conv_bias: float32 [96], replicated, may hold values from -0.5 to 0.5
- cotangent: float32 [96, 128, 8192], P(None, 'lat', 'lon'), may hold values from -6 to 6
Outputs:
- output_field: float32 [96, 128, 8192], P(None, 'lat', 'lon')
- field_grad: float32 [96, 128, 8192], P(None, 'lat', 'lon')
- weight_grad: float32 [96, 864], replicated
- bias_grad: float32 [96], replicated
The draws below stay inside these ranges and needn't reach their ends.
All inputs are finite; a program needn't handle non-finite values.
Results may differ from the reference program's by a relative error of at most 0.00012.
Values sent between devices are 32-bit elements; how exact they have to be, the bound alone decides.
No kernel may reach another device: no remote copies, remote signals or barrier semaphores. Data moves between devices by JAX's collectives and lax.ppermute only.
A program may use at most 64 MiB of HBM per device.

```python
import math
import jax
import jax.numpy as jnp
from jax import lax

C = 96
NROWS = 128
NCOLS = 8192


def steps_of(key, shape, cuts, least, top_value):
    factor_of = 1.0
    for dim, shards_of in cuts:
        steps = jax.random.uniform(jax.random.fold_in(jax.random.fold_in(key, 6), dim), (shards_of,), jnp.float32, least / len(cuts), top_value / len(cuts))
        factor_of = factor_of * jnp.repeat(jnp.exp(steps), shape[dim] // shards_of).reshape((-1,) + (1,) * (len(shape) - 1 - dim))
    return factor_of


def gaussian(stream_key, dims, width, limit, shards=(), dtype=jnp.bfloat16):
    result = width * jax.random.normal(stream_key, dims, jnp.float32)
    if shards:
        result = result * steps_of(stream_key, dims, shards, -0.22, 0.18)
    return jnp.clip(result, -limit, limit).astype(dtype)


def setup_inputs(seed: int = 0) -> dict:
    key_of = jax.random.split(jax.random.key(seed), 5)
    return {
        "input_field": gaussian(key_of[0], (C, NROWS, NCOLS), 1.0, 6.0, ((1, 8), (2, 64)), jnp.float32),
        "conv_weight": gaussian(key_of[1], (C, 9 * C), (9 * C) ** -0.5, 0.21875, (), jnp.float32),
        "conv_bias": jnp.clip(jax.random.uniform(key_of[2], (C,), jnp.float32, -0.5, 0.5), -0.5, 0.5),
        "cotangent": gaussian(key_of[3], (C, NROWS, NCOLS), 1.0, 6.0, ((1, 8), (2, 64)), jnp.float32),
    }


HIGHEST = lax.Precision.HIGHEST

def extend_grid(field):
    half_turn = field.shape[2] // 2
    rolled = jnp.roll(field, -half_turn, axis=2)
    with_rows = jnp.concatenate([rolled[:, 0:1, :], field, rolled[:, -1:, :]], axis=1)
    return jnp.concatenate([with_rows[:, :, -1:], with_rows, with_rows[:, :, :1]], axis=2)

def reference(input_field, conv_weight, conv_bias, cotangent):
    channels, row_count, col_count = input_field.shape
    padded_field = extend_grid(input_field)
    output_field = jnp.zeros(input_field.shape, jnp.float32) + conv_bias[:, None, None]
    weight_parts = []
    padded_grad = jnp.zeros(padded_field.shape, jnp.float32)
    for a in range(3):
        for b in range(3):
            kernel_tap = conv_weight[:, (3 * a + b) * channels:(3 * a + b + 1) * channels]
            window = padded_field[:, a:a + row_count, b:b + col_count]
            output_field = output_field + jnp.einsum('oi,irc->orc', kernel_tap, window, precision=HIGHEST)
            weight_parts.append(jnp.einsum('orc,irc->oi', cotangent, window, precision=HIGHEST))
            padded_grad = padded_grad.at[:, a:a + row_count, b:b + col_count].add(jnp.einsum('oi,orc->irc', kernel_tap, cotangent, precision=HIGHEST))
    adjoint = jax.vjp(extend_grid, input_field)[1]
    field_grad = adjoint(padded_grad)[0]
    factor = 1.0 / math.sqrt(row_count * col_count)
    weight_grad = jnp.concatenate(weight_parts, axis=1) * factor
    bias_grad = lax.optimization_barrier(jnp.sum(cotangent, axis=(1, 2))) * factor
    return (output_field, field_grad, weight_grad, bias_grad)
```

```python
import functools
import math

import jax
import jax.numpy as jnp
from jax import lax
from jax.experimental import pallas as pl
from jax.experimental.pallas import tpu as pltpu
from jax.sharding import Mesh
from jax.sharding import PartitionSpec as P

F32 = jnp.float32
BF16 = jnp.bfloat16
C = 96
R = 16
L = 128
NT = (((1,), (1,)), ((), ()))

AXES = ("lat", "xh", "zr", "zd", "c")
LON = ("xh", "zr", "zd", "c")
NEAR = ("lat", "xh", "zd", "c")
FAR = ("zr",)

VMEM = pl.BlockSpec(memory_space=pltpu.VMEM)
SMEM = pl.BlockSpec(memory_space=pltpu.SMEM)


def call(kernel, outs, args, scratch=(), flops=0, moved=0):
    return pl.pallas_call(
        kernel,
        out_shape=outs,
        in_specs=[SMEM] + [VMEM] * (len(args) - 1),
        out_specs=[VMEM] * len(outs),
        scratch_shapes=list(scratch),
        compiler_params=pltpu.CompilerParams(vmem_limit_bytes=40 * 1024 * 1024),
        cost_estimate=pl.CostEstimate(flops=flops, bytes_accessed=moved, transcendentals=0),
    )(*args)


def out(*shape):
    return jax.ShapeDtypeStruct(shape, F32)


def roll(value, by):
    by = by % L
    return value if by == 0 else pltpu.roll(value, by, 1)


def lanes():
    return lax.broadcasted_iota(jnp.int32, (C, L), 1)


def row(ref, r):
    return ref[pl.ds(r, C, stride=R), :]


def pick(flag, when_set, otherwise):
    return jnp.where(flag == 1, when_set, otherwise)


def split(value):
    high = value.astype(BF16)
    return high, (value - high.astype(F32)).astype(BF16)


def edges_kernel(flags, x, g, near_col, far_col, row_1, row_2):
    lane = lanes()
    east = jnp.zeros((C, L), F32)
    west = jnp.zeros((C, L), F32)
    for r in range(R):
        for ref, base in ((x, 0), (g, R)):
            here = row(ref, r)
            east = jnp.where(lane == base + r, roll(here, base + r + 1), east)
            west = jnp.where(lane == base + r, roll(here, base + r), west)
    near_col[...] = pick(flags[0], west, east)
    far_col[...] = pick(flags[0], east, west)
    top = row(g, 0)
    bottom = row(g, R - 1)
    row_1[...] = pick(flags[1], top, bottom)
    row_2[...] = pick(flags[1], bottom, top)


def corners_kernel(flags, x, near_col, far_col, msg_1, msg_2):
    lane = lanes()
    west = pick(flags[0], near_col[...], far_col[...])
    east = pick(flags[0], far_col[...], near_col[...])

    def corner(r):
        parts = ((west, r), (east, r), (west, R + r), (east, R + r))
        total = jnp.zeros((C, L), F32)
        for k, (source, at) in enumerate(parts):
            total = jnp.where(lane == k, roll(source, k - at), total)
        return total

    for part, (top, bottom) in enumerate(
        ((row(x, 0), row(x, R - 1)), (corner(0), corner(R - 1)))
    ):
        msg_1[part] = pick(flags[1], top, bottom)
        msg_2[part] = pick(flags[1], bottom, top)


def taps(value, west, west_lane, east, east_lane):
    lane = lanes()
    before = jnp.where(lane == 0, roll(west, -west_lane), roll(value, 1))
    after = jnp.where(lane == L - 1, roll(east, L - 1 - east_lane), roll(value, -1))
    return before, value, after


def weight_kernel(
    chunk, flags, x, g, near_col, far_col, row_1, row_2, packed, s_hi, s_lo, c_hi, c_lo
):
    west = pick(flags[0], near_col[...], far_col[...])
    east = pick(flags[0], far_col[...], near_col[...])
    north = pick(flags[1], row_1[...], row_2[...])
    south = pick(flags[1], row_2[...], row_1[...])
    at_top = flags[2].astype(F32)
    at_bottom = flags[3].astype(F32)
    total = jnp.zeros((C, L), F32)
    for r in range(R):
        at = pl.ds(r * L, L)
        for b, value in enumerate(taps(row(x, r), west, r, east, r)):
            s_hi[pl.ds(b * C, C), at], s_lo[pl.ds(b * C, C), at] = split(value)
        here = row(g, r)
        total = total + here
        below = row(g, r + 1) if r + 1 < R else south * (1.0 - at_bottom)
        above = row(g, r - 1) if r > 0 else north * (1.0 - at_top)
        if r == 0:
            below = below + north * at_top
        if r == R - 1:
            above = above + south * at_bottom
        for a, value in enumerate((below, here, above)):
            c_hi[pl.ds(a * C, C), at], c_lo[pl.ds(a * C, C), at] = split(value)

    def product(left, right):
        return lax.dot_general(left[...], right[...], NT, preferred_element_type=F32)

    grad = product(c_hi, s_hi) + product(c_hi, s_lo) + product(c_lo, s_hi)
    wide = jnp.concatenate(
        [grad[a * C : (a + 1) * C] for a in range(3)] + [jnp.zeros((C, 32), F32)], axis=1
    )
    bias = lax.dot_general(
        jnp.ones((8, L), F32), total, NT, preferred_element_type=F32, precision=lax.Precision.HIGHEST
    )
    bias = jnp.concatenate([bias, jnp.zeros((8, L - C), F32)], axis=1)

    def put(q, value):
        packed[q // chunk, :, pl.ds((q % chunk) * L, L)] = value

    q = 0
    for i in range(C // 8):
        for j in range(7):
            tile = wide[8 * i : 8 * i + 8, L * j : L * j + L]
            for s in range(8):
                put(q, tile[s : s + 1])
                q += 1
    put(q, bias[0:1])
    for rest in range(q + 1, packed.shape[0] * chunk):
        put(rest, jnp.zeros((1, L), F32))


def unpack_kernel(chunk, factor, flags, gathered, weight_grad, bias_grad):
    def get(q):
        return gathered[q // chunk, :, pl.ds((q % chunk) * L, L)] * factor

    q = 0
    for i in range(C // 8):
        for j in range(7):
            tile = jnp.concatenate([get(q + s) for s in range(8)], axis=0)
            width = min(L, 9 * C - L * j)
            weight_grad[pl.ds(8 * i, 8), pl.ds(L * j, width)] = tile[:, :width]
            q += 8
    bias_grad[...] = get(q)[:, :C]


def conv_kernel(
    is_grad, flags, field, near_col, far_col, row_1, row_2, msg_1, msg_2, weight, bias, result, hi, lo
):
    west = pick(flags[0], near_col[...], far_col[...])
    east = pick(flags[0], far_col[...], near_col[...])
    if is_grad:
        north = pick(flags[1], row_1[...], row_2[...])
        south = pick(flags[1], row_2[...], row_1[...])
    else:
        north = pick(flags[1], msg_1[0], msg_2[0])
        south = pick(flags[1], msg_2[0], msg_1[0])
    north_ends = pick(flags[1], msg_1[1], msg_2[1])
    south_ends = pick(flags[1], msg_2[1], msg_1[1])
    base = R if is_grad else 0
    end = 2 if is_grad else 0

    def shifts(r):
        if r < 0:
            return taps(north, north_ends, end, north_ends, end + 1)
        if r >= R:
            return taps(south, south_ends, end, south_ends, end + 1)
        return taps(row(field, r), west, base + r, east, base + r)

    def put(block, half, values):
        for b, value in enumerate(values):
            at = (pl.ds((3 * block + b) * C, C), pl.ds(half * L, L))
            hi[at], lo[at] = split(value)

    half = R // 2
    if is_grad:
        at_top = flags[2].astype(F32)
        at_bottom = flags[3].astype(F32)
        outer_top = shifts(-1)
        outer_bottom = shifts(R)
        put(0, 0, [v * (1.0 - at_top) for v in outer_top])
        put(0, 1, shifts(half - 1))
        put(1, 0, shifts(0))
        put(1, 1, shifts(half))
        put(2, 0, [v + o * at_top for v, o in zip(shifts(1), outer_top)])
        put(2, 1, shifts(half + 1))
        for r in range(half):
            put(3 + r, 0, shifts(r))
            put(3 + r, 1, shifts(r + half))
        k = 3 + half
        put(k, 0, shifts(half - 2))
        put(k, 1, [v + o * at_bottom for v, o in zip(shifts(R - 2), outer_bottom)])
        put(k + 1, 0, shifts(half - 1))
        put(k + 1, 1, shifts(R - 1))
        put(k + 2, 0, shifts(half))
        put(k + 2, 1, [v * (1.0 - at_bottom) for v in outer_bottom])
        starts = [0] + [2 + r for r in range(1, half - 1)] + [k]
    else:
        for j in range(half + 2):
            put(j, 0, shifts(j - 1))
            put(j, 1, shifts(j - 1 + half))
        starts = list(range(half))
    w_hi, w_lo = split(weight[...])
    both = jnp.concatenate([w_hi, w_lo], axis=0)
    for r, start in enumerate(starts):
        at = pl.ds(start * 3 * C, 9 * C)
        first = jnp.dot(both, hi[at, :], preferred_element_type=F32)
        second = jnp.dot(w_hi, lo[at, :], preferred_element_type=F32)
        value = first[:C] + first[C:] + second
        if not is_grad:
            value = value + bias[...]
        result[pl.ds(r, C, stride=R), :] = value[:, :L]
        result[pl.ds(r + half, C, stride=R), :] = value[:, L:]


def conv(is_grad, *args):
    blocks = 3 + R // 2 + 3 if is_grad else R // 2 + 2
    scratch = pltpu.VMEM((blocks * 3 * C, 2 * L), BF16)
    return call(
        functools.partial(conv_kernel, is_grad),
        [out(C * R, L)],
        args,
        [scratch, scratch],
        flops=6 * 9 * C * C * R * L,
        moved=3 * 4 * C * R * L,
    )[0]


def shards(nlat, nlon, factor, x, weight, bias, g):
    lat = lax.axis_index("lat")
    lon = lax.axis_index(LON)
    flags = jnp.stack([lon % 2, lat % 2, lat == 0, lat == nlat - 1]).astype(jnp.int32)
    x = x.reshape(C * R, L)
    g = g.reshape(C * R, L)

    def pairs_of(partner):
        pairs = []
        for i in range(nlat):
            for j in range(nlon):
                to_lat, to_lon = partner(i, j)
                pairs.append((i * nlon + j, to_lat * nlon + to_lon))
        return pairs

    def across_2(i, j):
        to = i + 1 if i % 2 else i - 1
        return (to, j) if 0 <= to < nlat else (i, (j + nlon // 2) % nlon)

    near = pairs_of(lambda i, j: (i, j ^ 1))
    far = pairs_of(lambda i, j: (i, (j + (1 if j % 2 else -1)) % nlon))
    first = pairs_of(lambda i, j: (i ^ 1, j))
    second = pairs_of(across_2)

    def send(value, pairs):
        return lax.ppermute(value, AXES, pairs)

    block = 4 * C * R * L
    near_col, far_col, row_1, row_2 = call(
        edges_kernel, [out(C, L)] * 4, (flags, x, g), flops=block, moved=2 * block
    )
    far_col = send(far_col, far)
    row_2 = send(row_2, second)
    row_1 = send(row_1, first)
    near_col = send(near_col, near)

    n_near = nlat * nlon // lax.axis_size(FAR)
    chunk = -(-(7 * C + 1) // n_near)
    packed = call(
        functools.partial(weight_kernel, chunk),
        [out(n_near, 1, chunk * L)],
        (flags, x, g, near_col, far_col, row_1, row_2),
        [pltpu.VMEM((3 * C, R * L), BF16)] * 4,
        flops=6 * 9 * C * C * R * L,
        moved=2 * block,
    )[0]

    near_col, far_col, packed, weight, bias = lax.optimization_barrier(
        (near_col, far_col, packed, weight, bias)
    )
    parts = lax.all_to_all(packed, NEAR, 0, 0)
    mine = jnp.sum(parts, axis=0, keepdims=True)
    n_far = lax.axis_size(FAR)
    mine = lax.all_to_all(jnp.broadcast_to(mine, (n_far, 1, chunk * L)), FAR, 0, 0)
    mine = jnp.sum(mine, axis=0, keepdims=True)
    gathered = lax.all_to_all(jnp.broadcast_to(mine, (n_near, 1, chunk * L)), NEAR, 0, 0)
    weight_grad, bias_grad = call(
        functools.partial(unpack_kernel, chunk, factor),
        [out(C, 9 * C), out(1, C)],
        (flags, gathered),
    )

    msg_1, msg_2 = call(
        corners_kernel, [out(2, C, L)] * 2, (flags, x, near_col, far_col), moved=block
    )
    msg_2 = send(msg_2, second)
    msg_1 = send(msg_1, first)
    flipped = weight.reshape(C, 3, 3, C)[:, ::-1, ::-1].transpose(3, 1, 2, 0).reshape(C, 9 * C)
    halo = (near_col, far_col, row_1, row_2, msg_1, msg_2)
    column = bias.reshape(C, 1)
    output = conv(False, flags, x, *halo, weight, column)
    grad = conv(True, flags, g, *halo, flipped, column)
    return (
        output.reshape(C, R, L),
        grad.reshape(C, R, L),
        weight_grad,
        bias_grad.reshape(C),
    )


def solution(mesh):
    nlat, nlon = mesh.shape["lat"], mesh.shape["lon"]
    fine = Mesh(mesh.devices.reshape(nlat, 2, nlon // 8, 2, 2), AXES)
    factor = 1.0 / math.sqrt(nlat * R * nlon * L)
    field = P(None, "lat", LON)
    return jax.shard_map(
        functools.partial(shards, nlat, nlon, factor),
        mesh=fine,
        in_specs=(field, P(), P(), field),
        out_specs=(field, field, P(), P()),
        check_vma=False,
    )
```

```python
import functools
import math

import jax
import jax.numpy as jnp
from jax import lax
from jax.experimental import pallas as pl
from jax.experimental.pallas import tpu as pltpu
from jax.sharding import Mesh
from jax.sharding import PartitionSpec as P

F32 = jnp.float32
BF16 = jnp.bfloat16
C = 96
R = 16
L = 128
HALF = L // 2
NT = (((1,), (1,)), ((), ()))

AXES = ("lat", "xh", "zr", "zd", "c")
LON = ("xh", "zr", "zd", "c")
NEAR = ("lat", "xh", "zd", "c")
FAR = ("zr",)

VMEM = pl.BlockSpec(memory_space=pltpu.VMEM)
ANY = pl.BlockSpec(memory_space=pl.ANY)


GRANT = (64 << 20) - 600 * 1024


def call(kernel, outs, args, scratch=(), after=(), specs=None, grant=40 << 20, flops=0, moved=0):
    def body(*refs):
        kernel(*refs[: len(args)], *refs[len(args) + len(after) :])

    return pl.pallas_call(
        body,
        out_shape=outs,
        in_specs=(specs or [VMEM] * len(args)) + [ANY] * len(after),
        out_specs=[VMEM] * len(outs),
        scratch_shapes=list(scratch),
        compiler_params=pltpu.CompilerParams(vmem_limit_bytes=grant),
        cost_estimate=pl.CostEstimate(flops=flops, bytes_accessed=moved, transcendentals=0),
    )(*args, *after)


def out(*shape):
    return jax.ShapeDtypeStruct(shape, F32)


def roll(value, by):
    by = by % L
    return value if by == 0 else pltpu.roll(value, by, 1)


def lanes():
    return lax.broadcasted_iota(jnp.int32, (C, L), 1)


def row(ref, r):
    return ref[pl.ds(r, C, stride=R), :]


def pick(flag, when_set, otherwise):
    return jnp.where(flag == 1, when_set, otherwise)


def split(value):
    high = value.astype(BF16)
    return high, (value - high.astype(F32)).astype(BF16)


def odd_lat():
    return lax.axis_index("lat") % 2


def at_end(place):
    return jnp.where(lax.axis_index("lat") == place, 1.0, 0.0)


def place_of(to):
    nlat = lax.axis_size("lat")
    half = lax.axis_index("xh")
    outside = jnp.logical_or(to < 0, to >= nlat)
    lat = jnp.clip(to, 0, nlat - 1)
    half = jnp.where(outside, 1 - half, half)
    return ((lat * 2 + half) * 2 + lax.axis_index("zd")) * 2 + lax.axis_index("c")


def lat_neighbours():
    lat = lax.axis_index("lat")
    return place_of(lat - 1), place_of(lat + 1)


class Chunks:
    CORNERS = 2

    def __init__(self, n):
        self.n = n
        self.tiles = 7 * C // 8
        self.rows = 4 * -(-(8 * self.tiles + 1) // (4 * n))

    def pieces(self, first, count):
        end = first + count
        while first < end:
            now = min(self.rows - first % self.rows, end - first)
            yield first // self.rows, first % self.rows, now
            first += now


PIECES = 4


def front_kernel(x, g, own_1, own_2, west, east, x_here, g_here, sems):
    step = C // PIECES
    copies = {}
    for k in range(PIECES):
        at = pl.ds(k * step * R, step * R)
        for part, (source, here) in enumerate(((x, x_here), (g, g_here))):
            copies[k, part] = pltpu.make_async_copy(source.at[at, :], here.at[at, :], sems.at[k, part])
            copies[k, part].start()
    odd = odd_lat()
    lane = lax.broadcasted_iota(jnp.int32, (step, L), 1)
    for k in range(PIECES):
        to = pl.ds(k * step, step)
        first = jnp.zeros((step, L), F32)
        last = jnp.zeros((step, L), F32)
        for part, here in enumerate((x_here, g_here)):
            copies[k, part].wait()
            base = HALF * part
            for r in range(R):
                value = here[pl.ds(k * step * R + r, step, stride=R), :]
                if r == 0:
                    top = value
                moved = roll(value, base + r + 1)
                last = jnp.where(lane == base + r, moved, last)
                first = jnp.where(lane == base + r + 1, moved, first)
            own_1[part, to, :] = pick(odd, top, value)
            own_2[part, to, :] = pick(odd, value, top)
        west[to, :] = roll(first, -1)
        east[to, :] = roll(last, 1)


def whole_column(east, row_1, row_2):
    lane = lanes()
    column = east[...]
    odd = odd_lat()
    for part in range(2):
        north = pick(odd, row_1[part], row_2[part])
        south = pick(odd, row_2[part], row_1[part])
        column = jnp.where(lane == HALF * part, roll(north, 1 + HALF * part), column)
        column = jnp.where(lane == HALF * part + R + 1, roll(south, HALF * part + R + 2), column)
    return column


def column_kernel(east, row_1, row_2, column):
    column[...] = whole_column(east, row_1, row_2)


def taps(value, west, west_lane, east, east_lane):
    lane = lanes()
    before = jnp.where(lane == 0, roll(west, -west_lane), roll(value, 1))
    after = jnp.where(lane == L - 1, roll(east, L - 1 - east_lane), roll(value, -1))
    return before, value, after


def nt(left, right):
    return lax.dot_general(left[...], right[...], NT, preferred_element_type=F32)


def three_products(c_hi, c_lo, s_hi, s_lo):
    grad = nt(c_hi, s_hi) + nt(c_hi, s_lo) + nt(c_lo, s_hi)
    return jnp.concatenate(
        [grad[a * C : (a + 1) * C] for a in range(3)] + [jnp.zeros((C, 7 * L - 9 * C), F32)], axis=1
    )


def inner_taps(value):
    lane = lanes()
    before = jnp.where(lane == 0, 0.0, roll(value, 1))
    after = jnp.where(lane == L - 1, 0.0, roll(value, -1))
    return before, value, after


def inner_weight_kernel(x, g, inner, bias, s_hi, s_lo, c_hi, c_lo):
    zero = jnp.zeros((C, L), F32)
    total = zero
    for r in range(R):
        at = pl.ds(r * L, L)
        for b, value in enumerate(inner_taps(row(x, r))):
            s_hi[pl.ds(b * C, C), at], s_lo[pl.ds(b * C, C), at] = split(value)
        here_hi, here_lo = split(row(g, r))
        total = total + row(g, r)
        for a in range(3):
            to = r + a - 1
            if 0 <= to < R:
                c_hi[pl.ds(a * C, C), pl.ds(to * L, L)] = here_hi
                c_lo[pl.ds(a * C, C), pl.ds(to * L, L)] = here_lo
    for a, to in ((0, R - 1), (2, 0)):
        c_hi[pl.ds(a * C, C), pl.ds(to * L, L)] = zero.astype(BF16)
        c_lo[pl.ds(a * C, C), pl.ds(to * L, L)] = zero.astype(BF16)
    inner[...] = three_products(c_hi, c_lo, s_hi, s_lo)
    bias[...] = jnp.zeros((8, L), F32)
    bias[:, pl.ds(0, C)] = lax.dot_general(
        jnp.ones((8, L), F32), total, NT, preferred_element_type=F32, precision=lax.Precision.HIGHEST
    )


def outer_weight_kernel(
    chunks, inner, bias, own_east, own_1, own_2, east, row_1, row_2, packed, s_hi, s_lo, c_hi, c_lo
):
    lane = lanes()
    zero = jnp.zeros((C, L), F32)
    odd = odd_lat()
    north = pick(odd, row_1[1], row_2[1])
    south = pick(odd, row_2[1], row_1[1])
    x_top = pick(odd, own_1[0], own_2[0])
    x_bottom = pick(odd, own_2[0], own_1[0])
    column = whole_column(own_east, row_1, row_2)
    beyond = east[...]
    at_top = at_end(0)
    at_bottom = at_end(lax.axis_size("lat") - 1)

    def put(k, left, right):
        at = pl.ds(k * L, L)
        for part, value in enumerate(left):
            c_hi[pl.ds(part * C, C), at], c_lo[pl.ds(part * C, C), at] = split(value)
        for part, value in enumerate(right):
            s_hi[pl.ds(part * C, C), at], s_lo[pl.ds(part * C, C), at] = split(value)

    put(0, (north * at_top, zero, north * (1.0 - at_top)), inner_taps(x_top))
    put(1, (south * (1.0 - at_bottom), zero, south * at_bottom), inner_taps(x_bottom))
    g_column = roll(column, -HALF)
    below = roll(g_column, -2)
    above = g_column
    south_end = jnp.where(lane == R - 1, below * at_bottom, 0.0)
    north_end = jnp.where(lane == 0, above * at_top, 0.0)
    put(
        2,
        (below - south_end + north_end, roll(g_column, -1), above - north_end + south_end),
        (zero, zero, jnp.where(lane < R, beyond, 0.0)),
    )
    g_beyond = jnp.where(lane < R, roll(beyond, -HALF), 0.0)
    put(
        3,
        (g_beyond, roll(g_beyond, 1), roll(g_beyond, 2)),
        (jnp.where(lane < R + 2, column, 0.0), zero, zero),
    )
    wide = inner[...] + three_products(c_hi, c_lo, s_hi, s_lo)
    height = chunks.rows + chunks.CORNERS
    for tile in range(chunks.tiles):
        i, j = divmod(tile, 7)
        at = 8 * i
        for chunk, place, count in chunks.pieces(8 * tile, 8):
            packed[pl.ds(chunk * height + place, count), :] = wide[at : at + count, L * j : L * j + L]
            at += count
    at = 0
    for chunk, place, count in chunks.pieces(8 * chunks.tiles, 8):
        packed[pl.ds(chunk * height + place, count), :] = bias[pl.ds(at, count), :]
        at += count
    for chunk, place, count in chunks.pieces(
        8 * chunks.tiles + 8, chunks.n * chunks.rows - 8 * chunks.tiles - 8
    ):
        packed[pl.ds(chunk * height + place, count), :] = jnp.zeros((count, L), F32)

    cells = zero
    for k, at in enumerate((0, HALF, R - 1, HALF + R - 1)):
        cells = jnp.where(lane == k, roll(beyond, k - at), cells)
    cells = jnp.concatenate([cells, jnp.zeros((L - C, L), F32)], axis=0).T
    to_north, to_south = lat_neighbours()
    for chunk in range(chunks.n):
        value = jnp.where(to_north == chunk, cells[0:2], 0.0)
        value = jnp.where(to_south == chunk, cells[2:4], value)
        packed[pl.ds(chunk * height + chunks.rows, chunks.CORNERS), :] = value


def unpack_kernel(tiles, factor, gathered, weight_grad, bias_grad):
    for tile in range(tiles):
        i, j = divmod(tile, 7)
        width = min(L, 9 * C - L * j)
        value = gathered[pl.ds(8 * tile, 8), :] * factor
        weight_grad[pl.ds(8 * i, 8), pl.ds(L * j, width)] = value[:, :width]
    bias_grad[...] = gathered[pl.ds(8 * tiles, 1), :][:, :C] * factor


def conv_kernel(
    is_grad, field, west, east, row_1, row_2, weight, bias, parts, result, token, hi, lo, ends, sems
):
    part = 1 if is_grad else 0
    copies = [
        pltpu.make_async_copy(
            parts.at[at, :, pl.ds(parts.shape[2] - 2 * L, 2 * L)], ends.at[k], sems.at[k]
        )
        for k, at in enumerate(lat_neighbours())
    ]
    for copy in copies:
        copy.start()
    odd = odd_lat()
    north = pick(odd, row_1[part], row_2[part])
    south = pick(odd, row_2[part], row_1[part])
    for copy in copies:
        copy.wait()
    corners = [ends[k][:, at : at + L] for k in range(2) for at in (0, L)]
    corners = jnp.concatenate(corners + [jnp.zeros((L - 4, L), F32)], axis=0).T[:C]
    first = HALF * part

    def shifts(r):
        if r < 0:
            return taps(north, west[...], first + r + 1, corners, part)
        if r >= R:
            return taps(south, west[...], first + r + 1, corners, 2 + part)
        return taps(row(field, r), west[...], first + r + 1, east[...], first + r)

    def put(block, half, values):
        for b, value in enumerate(values):
            at = (pl.ds((3 * block + b) * C, C), pl.ds(half * L, L))
            hi[at], lo[at] = split(value)

    half = R // 2
    if is_grad:
        at_top = at_end(0)
        at_bottom = at_end(lax.axis_size("lat") - 1)
        outer_top = shifts(-1)
        outer_bottom = shifts(R)
        put(0, 0, [v * (1.0 - at_top) for v in outer_top])
        put(0, 1, shifts(half - 1))
        put(1, 0, shifts(0))
        put(1, 1, shifts(half))
        put(2, 0, [v + o * at_top for v, o in zip(shifts(1), outer_top)])
        put(2, 1, shifts(half + 1))
        for r in range(half):
            put(3 + r, 0, shifts(r))
            put(3 + r, 1, shifts(r + half))
        k = 3 + half
        put(k, 0, shifts(half - 2))
        put(k, 1, [v + o * at_bottom for v, o in zip(shifts(R - 2), outer_bottom)])
        put(k + 1, 0, shifts(half - 1))
        put(k + 1, 1, shifts(R - 1))
        put(k + 2, 0, shifts(half))
        put(k + 2, 1, [v * (1.0 - at_bottom) for v in outer_bottom])
        starts = [0] + [2 + r for r in range(1, half - 1)] + [k]
    else:
        for j in range(half + 2):
            put(j, 0, shifts(j - 1))
            put(j, 1, shifts(j - 1 + half))
        starts = list(range(half))
    w_hi, w_lo = split(weight[...])
    both = jnp.concatenate([w_hi, w_lo], axis=0)
    for r, start in enumerate(starts):
        at = pl.ds(start * 3 * C, 9 * C)
        first = jnp.dot(both, hi[at, :], preferred_element_type=F32)
        second = jnp.dot(w_hi, lo[at, :], preferred_element_type=F32)
        value = first[:C] + first[C:] + second
        if not is_grad:
            value = value + bias[...]
        result[pl.ds(r, C, stride=R), :] = value[:, :L]
        result[pl.ds(r + half, C, stride=R), :] = value[:, L:]
    token[...] = jnp.zeros((8, L), F32)


def conv(is_grad, *args, after=()):
    blocks = 3 + R // 2 + 3 if is_grad else R // 2 + 2
    scratch = pltpu.VMEM((blocks * 3 * C, 2 * L), BF16)
    return call(
        functools.partial(conv_kernel, is_grad),
        [out(C * R, L), out(8, L)],
        args,
        [scratch, scratch, pltpu.VMEM((2, 1, 2 * L), F32), pltpu.SemaphoreType.DMA((2,))],
        after,
        specs=[VMEM] * (len(args) - 1) + [ANY],
        flops=6 * 9 * C * C * R * L,
        moved=3 * 4 * C * R * L,
    )


def shards(nlat, nlon, factor, x, weight, bias, g):
    x = x.reshape(C * R, L)
    g = g.reshape(C * R, L)

    def pairs_of(partner):
        pairs = []
        for i in range(nlat):
            for j in range(nlon):
                to_lat, to_lon = partner(i, j)
                pairs.append((i * nlon + j, to_lat * nlon + to_lon))
        return pairs

    def across_2(i, j):
        to = i + 1 if i % 2 else i - 1
        return (to, j) if 0 <= to < nlat else (i, (j + nlon // 2) % nlon)

    to_west = pairs_of(lambda i, j: (i, (j - 1) % nlon))
    to_east = pairs_of(lambda i, j: (i, (j + 1) % nlon))
    first = pairs_of(lambda i, j: (i ^ 1, j))
    second = pairs_of(across_2)

    def send(value, pairs):
        return lax.ppermute(value, AXES, pairs)

    block = 4 * C * R * L
    product = 6 * 9 * C * C * R * L
    own_1, own_2, own_west, own_east = call(
        front_kernel,
        [out(2, C, L)] * 2 + [out(C, L)] * 2,
        (x, g),
        [pltpu.VMEM((C * R, L), F32)] * 2 + [pltpu.SemaphoreType.DMA((PIECES, 2))],
        specs=[ANY] * 2,
        grant=GRANT,
        flops=block,
        moved=2 * block,
    )
    row_2 = send(own_2, second)
    row_1 = send(own_1, first)
    east = send(own_west, to_west)
    inner_sum, bias_sum = call(
        inner_weight_kernel,
        [out(C, 7 * L), out(8, L)],
        (x, g),
        [pltpu.VMEM((3 * C, R * L), BF16)] * 4,
        after=(own_west,),
        flops=product,
        moved=2 * block,
    )

    n_far = lax.axis_size(FAR)
    n_near = nlat * nlon // n_far
    chunks = Chunks(n_near)
    height = chunks.rows + chunks.CORNERS
    packed = call(
        functools.partial(outer_weight_kernel, chunks),
        [out(n_near * height, L)],
        (inner_sum, bias_sum, own_east, own_1, own_2, east, row_1, row_2),
        [pltpu.VMEM((3 * C, 4 * L), BF16)] * 4,
        flops=product // 4,
        moved=block,
    )[0]
    parts = lax.all_to_all(packed.reshape(n_near, 1, height * L), NEAR, 0, 0)
    column = call(column_kernel, [out(C, L)], (own_east, row_1, row_2), after=(packed,))[0]
    west = send(column, to_east)
    parts, west = lax.optimization_barrier((parts, west))
    mine = jnp.sum(parts[:, :, : chunks.rows * L], axis=0, keepdims=True)
    others = lax.all_to_all(jnp.broadcast_to(mine, (n_far, 1, chunks.rows * L)), FAR, 0, 0)
    flipped = weight.reshape(C, 3, 3, C)[:, ::-1, ::-1].transpose(3, 1, 2, 0).reshape(C, 9 * C)
    halo = (west, east, row_1, row_2)
    bias = bias.reshape(C, 1)
    output, token = conv(False, x, *halo, weight, bias, parts)
    others, token = lax.optimization_barrier((others, token))
    mine = jnp.sum(others, axis=0, keepdims=True)
    mine = jnp.broadcast_to(mine, (n_near, 1, chunks.rows * L))
    gathered = lax.all_to_all(mine, NEAR, 0, 0)
    grad, _ = conv(True, g, *halo, flipped, bias, parts, after=(mine,))
    weight_grad, bias_grad = call(
        functools.partial(unpack_kernel, chunks.tiles, factor),
        [out(C, 9 * C), out(1, C)],
        (gathered.reshape(n_near * chunks.rows, L),),
        moved=block,
    )
    return (
        output.reshape(C, R, L),
        grad.reshape(C, R, L),
        weight_grad,
        bias_grad.reshape(C),
    )


def solution(mesh):
    nlat, nlon = mesh.shape["lat"], mesh.shape["lon"]
    fine = Mesh(mesh.devices.reshape(nlat, 2, nlon // 8, 2, 2), AXES)
    factor = 1.0 / math.sqrt(nlat * R * nlon * L)
    field = P(None, "lat", LON)
    return jax.shard_map(
        functools.partial(shards, nlat, nlon, factor),
        mesh=fine,
        in_specs=(field, P(), P(), field),
        out_specs=(field, field, P(), P()),
        check_vma=False,
    )
```

```python
import functools
import math

import jax
import jax.numpy as jnp
from jax import lax
from jax.experimental import pallas as pl
from jax.experimental.pallas import tpu as pltpu
from jax.sharding import Mesh
from jax.sharding import PartitionSpec as P

F32 = jnp.float32
BF16 = jnp.bfloat16
C = 96
R = 16
L = 128
HALF = L // 2
NT = (((1,), (1,)), ((), ()))

AXES = ("lat", "xh", "zr", "zd", "c")
LON = ("xh", "zr", "zd", "c")
NEAR = ("lat", "xh", "zd", "c")
FAR = ("zr",)

VMEM = pl.BlockSpec(memory_space=pltpu.VMEM)
ANY = pl.BlockSpec(memory_space=pl.ANY)


def call(kernel, outs, args, scratch=(), after=(), specs=None, grant=40 << 20, flops=0, moved=0):
    def body(*refs):
        kernel(*refs[: len(args)], *refs[len(args) + len(after) :])

    return pl.pallas_call(
        body,
        out_shape=outs,
        in_specs=(specs or [VMEM] * len(args)) + [ANY] * len(after),
        out_specs=[VMEM] * len(outs),
        scratch_shapes=list(scratch),
        compiler_params=pltpu.CompilerParams(vmem_limit_bytes=grant),
        cost_estimate=pl.CostEstimate(flops=flops, bytes_accessed=moved, transcendentals=0),
    )(*args, *after)


def out(*shape):
    return jax.ShapeDtypeStruct(shape, F32)


def kept(*shape):
    return pltpu.VMEM(shape, F32)


def in_hbm(value):
    return pltpu.with_memory_space_constraint(value, pltpu.HBM)


def roll(value, by):
    by = by % L
    return value if by == 0 else pltpu.roll(value, by, 1)


def lanes():
    return lax.broadcasted_iota(jnp.int32, (C, L), 1)


def row(ref, r):
    return ref[pl.ds(r, C, stride=R), :]


def pick(flag, when_set, otherwise):
    return jnp.where(flag == 1, when_set, otherwise)


def split(value):
    high = value.astype(BF16)
    return high, (value - high.astype(F32)).astype(BF16)


def odd_lat():
    return lax.axis_index("lat") % 2


def at_end(place):
    return jnp.where(lax.axis_index("lat") == place, 1.0, 0.0)


class Chunks:
    def __init__(self, n):
        self.n = n
        self.tiles = 7 * C // 8
        self.rows = -(-(8 * self.tiles + 1) // n)


PIECES = 3


def stream(x, g, x_here, g_here, sems):
    size = C * R // PIECES
    copies = {}
    for k in range(PIECES):
        at = pl.ds(k * size, size)
        for part, (source, here) in enumerate(((x, x_here), (g, g_here))):
            copies[k, part] = pltpu.make_async_copy(source.at[at, :], here.at[at, :], sems.at[k, part])
            copies[k, part].start()
    return copies


def front_kernel(x, g, own_1, own_2, west, east, done, x_here, g_here, sems):
    step = C // PIECES
    copies = stream(x, g, x_here, g_here, sems)
    odd = odd_lat()
    lane = lax.broadcasted_iota(jnp.int32, (step, L), 1)
    for k in range(PIECES):
        to = pl.ds(k * step, step)
        first = jnp.zeros((step, L), F32)
        last = jnp.zeros((step, L), F32)
        for part, here in enumerate((x_here, g_here)):
            copies[k, part].wait()
            base = HALF * part
            for r in range(R):
                value = here[pl.ds(k * step * R + r, step, stride=R), :]
                if r == 0:
                    top = value
                moved = roll(value, base + r + 1)
                last = jnp.where(lane == base + r, moved, last)
                first = jnp.where(lane == base + r + 1, moved, first)
            own_1[part, to, :] = pick(odd, top, value)
            own_2[part, to, :] = pick(odd, value, top)
        west[to, :] = roll(first, -1)
        east[to, :] = roll(last, 1)
    done[...] = jnp.zeros((8, L), F32)


def whole_column(east, row_1, row_2):
    lane = lanes()
    column = east[...]
    odd = odd_lat()
    for part in range(2):
        north = pick(odd, row_1[part], row_2[part])
        south = pick(odd, row_2[part], row_1[part])
        column = jnp.where(lane == HALF * part, roll(north, 1 + HALF * part), column)
        column = jnp.where(lane == HALF * part + R + 1, roll(south, HALF * part + R + 2), column)
    return column


def columns_kernel(own_east, row_1, row_2, column, corners):
    column[...] = whole_column(own_east, row_1, row_2)
    lane = lanes()
    odd = odd_lat()
    value = jnp.zeros((C, L), F32)
    for part in range(2):
        north = pick(odd, row_1[part], row_2[part])
        south = pick(odd, row_2[part], row_1[part])
        value = jnp.where(lane == HALF * part, roll(north, HALF * part), value)
        value = jnp.where(lane == HALF * part + 1, roll(south, HALF * part + 1), value)
    corners[...] = value


def taps(value, west, west_lane, east, east_lane):
    lane = lanes()
    before = jnp.where(lane == 0, roll(west, -west_lane), roll(value, 1))
    after = jnp.where(lane == L - 1, roll(east, L - 1 - east_lane), roll(value, -1))
    return before, value, after


def nt(left, right):
    return lax.dot_general(left[...], right[...], NT, preferred_element_type=F32)


def wide_form(grad):
    return jnp.concatenate(
        [grad[a * C : (a + 1) * C] for a in range(3)] + [jnp.zeros((C, 7 * L - 9 * C), F32)], axis=1
    )


def inner_taps(value):
    lane = lanes()
    before = jnp.where(lane == 0, 0.0, roll(value, 1))
    after = jnp.where(lane == L - 1, 0.0, roll(value, -1))
    return before, value, after


def inner_weight_kernel(x, g, inner, bias, x_here, g_here, sems, s_both, c_hi, c_lo):
    step = C // PIECES
    copies = stream(x, g, x_here, g_here, sems)
    lane = lax.broadcasted_iota(jnp.int32, (step, L), 1)
    zero = jnp.zeros((C, L), BF16)
    for a, to in ((0, R - 1), (2, 0)):
        c_hi[pl.ds(a * C, C), pl.ds(to * L, L)] = zero
        c_lo[pl.ds(a * C, C), pl.ds(to * L, L)] = zero
    totals = []
    for k in range(PIECES):
        copies[k, 0].wait()
        for r in range(R):
            at = pl.ds(r * L, L)
            value = x_here[pl.ds(k * step * R + r, step, stride=R), :]
            before = jnp.where(lane == 0, 0.0, roll(value, 1))
            after = jnp.where(lane == L - 1, 0.0, roll(value, -1))
            for b, shifted in enumerate((before, value, after)):
                high, low = split(shifted)
                s_both[pl.ds(b * C + k * step, step), at] = high
                s_both[pl.ds((3 + b) * C + k * step, step), at] = low
        copies[k, 1].wait()
        total = jnp.zeros((step, L), F32)
        for r in range(R):
            value = g_here[pl.ds(k * step * R + r, step, stride=R), :]
            total = total + value
            high, low = split(value)
            for a in range(3):
                to = r + a - 1
                if 0 <= to < R:
                    c_hi[pl.ds(a * C + k * step, step), pl.ds(to * L, L)] = high
                    c_lo[pl.ds(a * C + k * step, step), pl.ds(to * L, L)] = low
        totals.append(total)
    both = nt(c_hi, s_both)
    inner[...] = wide_form(both[:, : 3 * C] + both[:, 3 * C :] + nt(c_lo, s_both.at[pl.ds(0, 3 * C), :]))
    bias[...] = jnp.zeros((8, L), F32)
    bias[:, pl.ds(0, C)] = lax.dot_general(
        jnp.ones((8, L), F32),
        jnp.concatenate(totals, axis=0),
        NT,
        preferred_element_type=F32,
        precision=lax.Precision.HIGHEST,
    )


def outer_weight_kernel(
    chunks, inner, bias, own_east, own_1, own_2, east, row_1, row_2, packed, s_hi, s_lo, c_hi, c_lo
):
    lane = lanes()
    zero = jnp.zeros((C, L), F32)
    odd = odd_lat()
    north = pick(odd, row_1[1], row_2[1])
    south = pick(odd, row_2[1], row_1[1])
    x_top = pick(odd, own_1[0], own_2[0])
    x_bottom = pick(odd, own_2[0], own_1[0])
    column = whole_column(own_east, row_1, row_2)
    beyond = east[...]
    at_top = at_end(0)
    at_bottom = at_end(lax.axis_size("lat") - 1)

    def put(k, left, right):
        at = pl.ds(k * L, L)
        for part, value in enumerate(left):
            c_hi[pl.ds(part * C, C), at], c_lo[pl.ds(part * C, C), at] = split(value)
        for part, value in enumerate(right):
            s_hi[pl.ds(part * C, C), at], s_lo[pl.ds(part * C, C), at] = split(value)

    put(0, (north * at_top, zero, north * (1.0 - at_top)), inner_taps(x_top))
    put(1, (south * (1.0 - at_bottom), zero, south * at_bottom), inner_taps(x_bottom))
    g_column = roll(column, -HALF)
    below = roll(g_column, -2)
    above = g_column
    south_end = jnp.where(lane == R - 1, below * at_bottom, 0.0)
    north_end = jnp.where(lane == 0, above * at_top, 0.0)
    put(
        2,
        (below - south_end + north_end, roll(g_column, -1), above - north_end + south_end),
        (zero, zero, jnp.where(lane < R, beyond, 0.0)),
    )
    g_beyond = jnp.where(lane < R, roll(beyond, -HALF), 0.0)
    put(
        3,
        (g_beyond, roll(g_beyond, 1), roll(g_beyond, 2)),
        (jnp.where(lane < R + 2, column, 0.0), zero, zero),
    )
    wide = inner[...] + wide_form(nt(c_hi, s_hi) + nt(c_hi, s_lo) + nt(c_lo, s_hi))
    for tile in range(chunks.tiles):
        i, j = divmod(tile, 7)
        packed[pl.ds(8 * tile, 8), :] = wide[8 * i : 8 * i + 8, L * j : L * j + L]
    at = 8 * chunks.tiles
    packed[pl.ds(at, 8), :] = bias[...]
    rest = packed.shape[0] - at - 8
    packed[pl.ds(at + 8, rest), :] = jnp.zeros((rest, L), F32)


def sum_kernel(parts, result):
    total = parts[0]
    for k in range(1, parts.shape[0]):
        total = total + parts[k]
    for k in range(result.shape[0]):
        result[k] = total


def unpack_kernel(tiles, factor, gathered, weight_grad, bias_grad):
    for tile in range(tiles):
        i, j = divmod(tile, 7)
        width = min(L, 9 * C - L * j)
        value = gathered[pl.ds(8 * tile, 8), :] * factor
        weight_grad[pl.ds(8 * i, 8), pl.ds(L * j, width)] = value[:, :width]
    bias_grad[...] = gathered[pl.ds(8 * tiles, 1), :][:, :C] * factor


def conv_kernel(
    is_grad, field, west, east, corners, row_1, row_2, weight, bias, result, token, hi, lo
):
    part = 1 if is_grad else 0
    odd = odd_lat()
    north = pick(odd, row_1[part], row_2[part])
    south = pick(odd, row_2[part], row_1[part])
    first = HALF * part

    def shifts(r):
        if r < 0:
            return taps(north, west[...], first + r + 1, corners[...], first)
        if r >= R:
            return taps(south, west[...], first + r + 1, corners[...], first + 1)
        return taps(row(field, r), west[...], first + r + 1, east[...], first + r)

    def put(block, half, values):
        for b, value in enumerate(values):
            at = (pl.ds((3 * block + b) * C, C), pl.ds(half * L, L))
            hi[at], lo[at] = split(value)

    half = R // 2
    if is_grad:
        at_top = at_end(0)
        at_bottom = at_end(lax.axis_size("lat") - 1)
        outer_top = shifts(-1)
        outer_bottom = shifts(R)
        put(0, 0, [v * (1.0 - at_top) for v in outer_top])
        put(0, 1, shifts(half - 1))
        put(1, 0, shifts(0))
        put(1, 1, shifts(half))
        put(2, 0, [v + o * at_top for v, o in zip(shifts(1), outer_top)])
        put(2, 1, shifts(half + 1))
        for r in range(half):
            put(3 + r, 0, shifts(r))
            put(3 + r, 1, shifts(r + half))
        k = 3 + half
        put(k, 0, shifts(half - 2))
        put(k, 1, [v + o * at_bottom for v, o in zip(shifts(R - 2), outer_bottom)])
        put(k + 1, 0, shifts(half - 1))
        put(k + 1, 1, shifts(R - 1))
        put(k + 2, 0, shifts(half))
        put(k + 2, 1, [v * (1.0 - at_bottom) for v in outer_bottom])
        starts = [0] + [2 + r for r in range(1, half - 1)] + [k]
    else:
        for j in range(half + 2):
            put(j, 0, shifts(j - 1))
            put(j, 1, shifts(j - 1 + half))
        starts = list(range(half))
    w_hi, w_lo = split(weight[...])
    both = jnp.concatenate([w_hi, w_lo], axis=0)
    for r, start in enumerate(starts):
        at = pl.ds(start * 3 * C, 9 * C)
        first = jnp.dot(both, hi[at, :], preferred_element_type=F32)
        second = jnp.dot(w_hi, lo[at, :], preferred_element_type=F32)
        value = first[:C] + first[C:] + second
        if not is_grad:
            value = value + bias[...]
        result[pl.ds(r, C, stride=R), :] = value[:, :L]
        result[pl.ds(r + half, C, stride=R), :] = value[:, L:]
    token[...] = jnp.zeros((8, L), F32)


def conv(is_grad, *args, after=()):
    blocks = 3 + R // 2 + 3 if is_grad else R // 2 + 2
    scratch = pltpu.VMEM((blocks * 3 * C, 2 * L), BF16)
    return call(
        functools.partial(conv_kernel, is_grad),
        [out(C * R, L), out(8, L)],
        args,
        [scratch, scratch],
        after,
        flops=4 * 6 * 9 * C * C * R * L,
        moved=3 * 4 * C * R * L,
    )


def shards(nlat, nlon, factor, x, weight, bias, g):
    x = x.reshape(C * R, L)
    g = g.reshape(C * R, L)

    def pairs_of(partner):
        pairs = []
        for i in range(nlat):
            for j in range(nlon):
                to_lat, to_lon = partner(i, j)
                pairs.append((i * nlon + j, to_lat * nlon + to_lon))
        return pairs

    def across_2(i, j):
        to = i + 1 if i % 2 else i - 1
        return (to, j) if 0 <= to < nlat else (i, (j + nlon // 2) % nlon)

    to_west = pairs_of(lambda i, j: (i, (j - 1) % nlon))
    to_east = pairs_of(lambda i, j: (i, (j + 1) % nlon))
    first = pairs_of(lambda i, j: (i ^ 1, j))
    second = pairs_of(across_2)

    def send(value, pairs):
        return lax.ppermute(value, AXES, pairs)

    block = 4 * C * R * L
    product = 6 * 9 * C * C * R * L
    own_1, own_2, own_west, own_east, done = call(
        front_kernel,
        [kept(2, C, L)] * 2 + [kept(C, L)] * 2 + [kept(8, L)],
        (in_hbm(x), in_hbm(g)),
        [pltpu.VMEM((C * R, L), F32)] * 2 + [pltpu.SemaphoreType.DMA((PIECES, 2))],
        specs=[ANY] * 2,
        flops=block,
        moved=2 * block,
    )
    row_2 = send(own_2, second)
    row_1 = send(own_1, first)
    east = send(own_west, to_west)
    inner_sum, bias_sum = call(
        inner_weight_kernel,
        [out(C, 7 * L), out(8, L)],
        (in_hbm(x), in_hbm(g)),
        [pltpu.VMEM((C * R, L), F32)] * 2
        + [pltpu.SemaphoreType.DMA((PIECES, 2)), pltpu.VMEM((6 * C, R * L), BF16)]
        + [pltpu.VMEM((3 * C, R * L), BF16)] * 2,
        after=(done,),
        specs=[ANY] * 2,
        flops=product,
        moved=2 * block,
    )

    n_far = lax.axis_size(FAR)
    n_near = nlat * nlon // n_far
    chunks = Chunks(n_near)
    packed = call(
        functools.partial(outer_weight_kernel, chunks),
        [kept(n_near * chunks.rows, L)],
        (inner_sum, bias_sum, own_east, own_1, own_2, east, row_1, row_2),
        [pltpu.VMEM((3 * C, 4 * L), BF16)] * 4,
        flops=product // 4,
        moved=block,
    )[0]
    parts = lax.all_to_all(packed.reshape(n_near, 1, chunks.rows * L), NEAR, 0, 0)
    column, ends = call(
        columns_kernel, [kept(C, L)] * 2, (own_east, row_1, row_2), after=(packed,)
    )
    west = send(column, to_east)
    corners = send(ends, to_west)
    mine = call(
        sum_kernel,
        [kept(n_far, 1, chunks.rows * L)],
        (parts,),
        after=(column, ends),
        moved=block // 2,
    )[0]
    others = lax.all_to_all(mine, FAR, 0, 0)
    flipped = weight.reshape(C, 3, 3, C)[:, ::-1, ::-1].transpose(3, 1, 2, 0).reshape(C, 9 * C)
    halo = (west, east, corners, row_1, row_2)
    bias = bias.reshape(C, 1)
    output, token = conv(False, x, *halo, weight, bias)
    mine = call(
        sum_kernel, [kept(n_near, 1, chunks.rows * L)], (others,), after=(token,), moved=block // 2
    )[0]
    gathered = lax.all_to_all(mine, NEAR, 0, 0)
    grad, _ = conv(True, g, *halo, flipped, bias, after=(mine,))
    weight_grad, bias_grad = call(
        functools.partial(unpack_kernel, chunks.tiles, factor),
        [out(C, 9 * C), out(1, C)],
        (gathered.reshape(n_near * chunks.rows, L),),
        moved=block,
    )
    return (
        output.reshape(C, R, L),
        grad.reshape(C, R, L),
        weight_grad,
        bias_grad.reshape(C),
    )


def solution(mesh):
    nlat, nlon = mesh.shape["lat"], mesh.shape["lon"]
    fine = Mesh(mesh.devices.reshape(nlat, 2, nlon // 8, 2, 2), AXES)
    factor = 1.0 / math.sqrt(nlat * R * nlon * L)
    field = P(None, "lat", LON)
    return jax.shard_map(
        functools.partial(shards, nlat, nlon, factor),
        mesh=fine,
        in_specs=(field, P(), P(), field),
        out_specs=(field, field, P(), P()),
        check_vma=False,
    )
```

```python
import functools
import math

import jax
import jax.numpy as jnp
from jax import lax
from jax.experimental import pallas as pl
from jax.experimental.pallas import tpu as pltpu
from jax.sharding import Mesh
from jax.sharding import PartitionSpec as P

F32 = jnp.float32
BF16 = jnp.bfloat16
C = 96
R = 16
L = 128
HALF = L // 2
NT = (((1,), (1,)), ((), ()))

AXES = ("lat", "xh", "zr", "zd", "c")
LON = ("xh", "zr", "zd", "c")
NEAR = ("lat", "xh", "zd", "c")
FAR = ("zr",)

VMEM = pl.BlockSpec(memory_space=pltpu.VMEM)
ANY = pl.BlockSpec(memory_space=pl.ANY)


def call(kernel, outs, args, scratch=(), after=(), specs=None, grant=40 << 20, flops=0, moved=0):
    def body(*refs):
        kernel(*refs[: len(args)], *refs[len(args) + len(after) :])

    return pl.pallas_call(
        body,
        out_shape=outs,
        in_specs=(specs or [VMEM] * len(args)) + [ANY] * len(after),
        out_specs=[VMEM] * len(outs),
        scratch_shapes=list(scratch),
        compiler_params=pltpu.CompilerParams(vmem_limit_bytes=grant),
        cost_estimate=pl.CostEstimate(flops=flops, bytes_accessed=moved, transcendentals=0),
    )(*args, *after)


def out(*shape):
    return jax.ShapeDtypeStruct(shape, F32)


def kept(*shape):
    return pltpu.VMEM(shape, F32)


def in_hbm(value):
    return pltpu.with_memory_space_constraint(value, pltpu.HBM)


def roll(value, by):
    by = by % L
    return value if by == 0 else pltpu.roll(value, by, 1)


def lanes():
    return lax.broadcasted_iota(jnp.int32, (C, L), 1)


def row(ref, r):
    return ref[pl.ds(r, C, stride=R), :]


def pick(flag, when_set, otherwise):
    return jnp.where(flag == 1, when_set, otherwise)


def split(value):
    high = value.astype(BF16)
    return high, (value - high.astype(F32)).astype(BF16)


def odd_lat():
    return lax.axis_index("lat") % 2


def at_end(place):
    return jnp.where(lax.axis_index("lat") == place, 1.0, 0.0)


def place_of(to):
    nlat = lax.axis_size("lat")
    half = lax.axis_index("xh")
    outside = jnp.logical_or(to < 0, to >= nlat)
    lat = jnp.clip(to, 0, nlat - 1)
    half = jnp.where(outside, 1 - half, half)
    return ((lat * 2 + half) * 2 + lax.axis_index("zd")) * 2 + lax.axis_index("c")


def lat_neighbours():
    lat = lax.axis_index("lat")
    return place_of(lat - 1), place_of(lat + 1)


TILES = 7 * C // 8


class Chunks:
    def __init__(self, n):
        self.n = n
        self.full = 8 * TILES // n
        self.rows = self.full + 1
        self.sent = self.full + 2
        self.halves = 8 * TILES - self.full * n
        assert self.halves in (0, n // 2) and self.full * n % 8 == 0

    def pieces(self, tile):
        at, end = 8 * tile, 8 * tile + 8
        while at < end:
            now = min(self.full - at % self.full, end - at)
            yield at // self.full, at % self.full, now
            at += now


PIECES = 3


def front_kernel(x, g, own_1, own_2, west, east, x_here, g_here, sems):
    step = C // PIECES
    copies = {}
    for k in range(PIECES):
        at = pl.ds(k * step * R, step * R)
        for part, (source, here) in enumerate(((x, x_here), (g, g_here))):
            copies[k, part] = pltpu.make_async_copy(source.at[at, :], here.at[at, :], sems.at[k, part])
            copies[k, part].start()
    odd = odd_lat()
    lane = lax.broadcasted_iota(jnp.int32, (step, L), 1)
    for k in range(PIECES):
        to = pl.ds(k * step, step)
        first = jnp.zeros((step, L), F32)
        last = jnp.zeros((step, L), F32)
        for part, here in enumerate((x_here, g_here)):
            copies[k, part].wait()
            base = HALF * part
            for r in range(R):
                value = here[pl.ds(k * step * R + r, step, stride=R), :]
                if r == 0:
                    top = value
                moved = roll(value, base + r + 1)
                last = jnp.where(lane == base + r, moved, last)
                first = jnp.where(lane == base + r + 1, moved, first)
            own_1[part, to, :] = pick(odd, top, value)
            own_2[part, to, :] = pick(odd, value, top)
        west[to, :] = roll(first, -1)
        east[to, :] = roll(last, 1)


def whole_column(east, row_1, row_2):
    lane = lanes()
    column = east[...]
    odd = odd_lat()
    for part in range(2):
        north = pick(odd, row_1[part], row_2[part])
        south = pick(odd, row_2[part], row_1[part])
        column = jnp.where(lane == HALF * part, roll(north, 1 + HALF * part), column)
        column = jnp.where(lane == HALF * part + R + 1, roll(south, HALF * part + R + 2), column)
    return column


def column_kernel(east, row_1, row_2, column):
    column[...] = whole_column(east, row_1, row_2)


def taps(value, west, west_lane, east, east_lane):
    lane = lanes()
    before = jnp.where(lane == 0, roll(west, -west_lane), roll(value, 1))
    after = jnp.where(lane == L - 1, roll(east, L - 1 - east_lane), roll(value, -1))
    return before, value, after


def nt(left, right):
    return lax.dot_general(left[...], right[...], NT, preferred_element_type=F32)


def wide_form(grad, bias):
    return jnp.concatenate(
        [grad[a * C : (a + 1) * C] for a in range(3)]
        + [bias, jnp.zeros((C, 7 * L - 9 * C - bias.shape[1]), F32)],
        axis=1,
    )


def inner_taps(value):
    lane = lanes()
    before = jnp.where(lane == 0, 0.0, roll(value, 1))
    after = jnp.where(lane == L - 1, 0.0, roll(value, -1))
    return before, value, after


def inner_weight_kernel(x, g, inner, s_both, c_hi, c_lo):
    zero = jnp.zeros((C, L), F32)
    total = zero
    for a, to in ((0, R - 1), (2, 0)):
        c_hi[pl.ds(a * C, C), pl.ds(to * L, L)] = zero.astype(BF16)
        c_lo[pl.ds(a * C, C), pl.ds(to * L, L)] = zero.astype(BF16)
    for r in range(R):
        at = pl.ds(r * L, L)
        for b, shifted in enumerate(inner_taps(row(x, r))):
            s_both[pl.ds(b * C, C), at], s_both[pl.ds((3 + b) * C, C), at] = split(shifted)
        value = row(g, r)
        total = total + value
        high, low = split(value)
        for a in range(3):
            to = r + a - 1
            if 0 <= to < R:
                c_hi[pl.ds(a * C, C), pl.ds(to * L, L)] = high
                c_lo[pl.ds(a * C, C), pl.ds(to * L, L)] = low
    both = nt(c_hi, s_both)
    grad = both[:, : 3 * C] + both[:, 3 * C :] + nt(c_lo, s_both.at[pl.ds(0, 3 * C), :])
    inner[...] = wide_form(grad, jnp.sum(total, axis=1, keepdims=True))


def outer_weight_kernel(
    chunks, inner, own_east, own_1, own_2, east, row_1, row_2, packed, s_hi, s_lo, c_hi, c_lo
):
    lane = lanes()
    zero = jnp.zeros((C, L), F32)
    odd = odd_lat()
    north = pick(odd, row_1[1], row_2[1])
    south = pick(odd, row_2[1], row_1[1])
    x_top = pick(odd, own_1[0], own_2[0])
    x_bottom = pick(odd, own_2[0], own_1[0])
    column = whole_column(own_east, row_1, row_2)
    beyond = east[...]
    at_top = at_end(0)
    at_bottom = at_end(lax.axis_size("lat") - 1)

    def put(k, left, right):
        at = pl.ds(k * L, L)
        for part, value in enumerate(left):
            c_hi[pl.ds(part * C, C), at], c_lo[pl.ds(part * C, C), at] = split(value)
        for part, value in enumerate(right):
            s_hi[pl.ds(part * C, C), at], s_lo[pl.ds(part * C, C), at] = split(value)

    put(0, (north * at_top, zero, north * (1.0 - at_top)), inner_taps(x_top))
    put(1, (south * (1.0 - at_bottom), zero, south * at_bottom), inner_taps(x_bottom))
    g_column = roll(column, -HALF)
    below = roll(g_column, -2)
    above = g_column
    south_end = jnp.where(lane == R - 1, below * at_bottom, 0.0)
    north_end = jnp.where(lane == 0, above * at_top, 0.0)
    put(
        2,
        (below - south_end + north_end, roll(g_column, -1), above - north_end + south_end),
        (zero, zero, jnp.where(lane < R, beyond, 0.0)),
    )
    g_beyond = jnp.where(lane < R, roll(beyond, -HALF), 0.0)
    put(
        3,
        (g_beyond, roll(g_beyond, 1), roll(g_beyond, 2)),
        (jnp.where(lane < R + 2, column, 0.0), zero, zero),
    )
    grad = nt(c_hi, s_hi) + nt(c_hi, s_lo) + nt(c_lo, s_hi)
    wide = inner[...] + wide_form(grad, jnp.zeros((C, 1), F32))
    cells = zero
    for k, at in enumerate((0, HALF, R - 1, HALF + R - 1)):
        cells = jnp.where(lane == k, roll(beyond, k - at), cells)
    cells = jnp.concatenate([cells, jnp.zeros((L - C, L), F32)], axis=0).T
    x_cells = roll(cells[0:8], HALF)
    g_cells = roll(cells[0:8], L // 4)
    lane = lax.broadcasted_iota(jnp.int32, (1, L), 1)
    corners = []
    for k in (0, 2):
        moved = x_cells[k : k + 1]
        corners.append((moved, jnp.where(lane < L // 4, moved, g_cells[k + 1 : k + 2])))
    to_north, to_south = lat_neighbours()
    left = chunks.full * chunks.n // 8
    for tile in range(TILES):
        i, j = divmod(tile, 7)
        value = wide[8 * i : 8 * i + 8, L * j : L * j + L]
        if tile < left:
            at = 0
            for chunk, place, count in chunks.pieces(tile):
                packed[pl.ds(chunk * chunks.sent + place, count), :] = value[at : at + count]
                at += count
        else:
            for k, half in enumerate((value, roll(value, HALF))):
                for r in range(8):
                    chunk = 2 * (8 * (tile - left) + r) + k
                    packed[pl.ds(chunk * chunks.sent + chunks.full, 1), :] = half[r : r + 1]
    for chunk in range(chunks.n):
        at = chunk * chunks.sent + chunks.full
        first = jnp.where(to_north == chunk, corners[0][0], jnp.where(to_south == chunk, corners[1][0], 0.0))
        if chunks.halves:
            first = jnp.where(lane < HALF, packed[pl.ds(at, 1), :], first)
        packed[pl.ds(at, 1), :] = first
        packed[pl.ds(at + 1, 1), :] = jnp.where(
            to_north == chunk, corners[0][1], jnp.where(to_south == chunk, corners[1][1], 0.0)
        )


def sum_kernel(rows, height, parts, result):
    total = parts[pl.ds(0, rows), :]
    for k in range(1, parts.shape[0] // height):
        total = total + parts[pl.ds(k * height, rows), :]
    for k in range(result.shape[0] // rows):
        result[pl.ds(k * rows, rows), :] = total


def unpack_kernel(chunks, factor, gathered, weight_grad, bias_grad):
    lane = lax.broadcasted_iota(jnp.int32, (8, L), 1)
    left = chunks.full * chunks.n // 8
    ends = []
    for tile in range(TILES):
        i, j = divmod(tile, 7)
        if tile < left:
            value = jnp.concatenate(
                [
                    gathered[pl.ds(chunk * chunks.rows + place, count), :]
                    for chunk, place, count in chunks.pieces(tile)
                ],
                axis=0,
            )
        else:
            at = 16 * (tile - left) * chunks.rows + chunks.full
            even, odd = (
                gathered[pl.ds(at + k * chunks.rows, 8, stride=2 * chunks.rows), :] for k in range(2)
            )
            value = jnp.where(lane < HALF, even, roll(odd, HALF))
        width = min(L, 9 * C - L * j)
        weight_grad[pl.ds(8 * i, 8), pl.ds(L * j, width)] = value[:, :width] * factor
        if width < L:
            ends.append(value)
    ends = jnp.concatenate(ends + [jnp.zeros((L - C, L), F32)], axis=0).T
    at = 9 * C % L
    bias_grad[...] = ends[at : at + 1, :C] * factor


def conv_kernel(
    is_grad, field, west, east, row_1, row_2, weight, bias, parts, result, token, hi, lo, ends, sems
):
    part = 1 if is_grad else 0
    copies = [
        pltpu.make_async_copy(
            parts.at[at, :, pl.ds(parts.shape[2] - 2 * L, 2 * L)], ends.at[k], sems.at[k]
        )
        for k, at in enumerate(lat_neighbours())
    ]
    for copy in copies:
        copy.start()
    odd = odd_lat()
    north = pick(odd, row_1[part], row_2[part])
    south = pick(odd, row_2[part], row_1[part])
    for copy in copies:
        copy.wait()
    lane = lax.broadcasted_iota(jnp.int32, (1, L), 1)
    corners = []
    for k in range(2):
        former, latter = ends[k][:, :L], ends[k][:, L:]
        if is_grad:
            corners.append(roll(latter, -(L // 4)))
        else:
            corners.append(jnp.where(lane < HALF, roll(former, HALF), roll(latter, HALF)))
    corners = jnp.concatenate(corners + [jnp.zeros((L - 2, L), F32)], axis=0).T[:C]
    first = HALF * part

    def shifts(r):
        if r < 0:
            return taps(north, west[...], first + r + 1, corners, 0)
        if r >= R:
            return taps(south, west[...], first + r + 1, corners, 1)
        return taps(row(field, r), west[...], first + r + 1, east[...], first + r)

    def put(block, half, values):
        for b, value in enumerate(values):
            at = (pl.ds((3 * block + b) * C, C), pl.ds(half * L, L))
            hi[at], lo[at] = split(value)

    half = R // 2
    if is_grad:
        at_top = at_end(0)
        at_bottom = at_end(lax.axis_size("lat") - 1)
        outer_top = shifts(-1)
        outer_bottom = shifts(R)
        put(0, 0, [v * (1.0 - at_top) for v in outer_top])
        put(0, 1, shifts(half - 1))
        put(1, 0, shifts(0))
        put(1, 1, shifts(half))
        put(2, 0, [v + o * at_top for v, o in zip(shifts(1), outer_top)])
        put(2, 1, shifts(half + 1))
        for r in range(half):
            put(3 + r, 0, shifts(r))
            put(3 + r, 1, shifts(r + half))
        k = 3 + half
        put(k, 0, shifts(half - 2))
        put(k, 1, [v + o * at_bottom for v, o in zip(shifts(R - 2), outer_bottom)])
        put(k + 1, 0, shifts(half - 1))
        put(k + 1, 1, shifts(R - 1))
        put(k + 2, 0, shifts(half))
        put(k + 2, 1, [v * (1.0 - at_bottom) for v in outer_bottom])
        starts = [0] + [2 + r for r in range(1, half - 1)] + [k]
    else:
        for j in range(half + 2):
            put(j, 0, shifts(j - 1))
            put(j, 1, shifts(j - 1 + half))
        starts = list(range(half))
    w_hi, w_lo = split(weight[...])
    both = jnp.concatenate([w_hi, w_lo], axis=0)
    for r, start in enumerate(starts):
        at = pl.ds(start * 3 * C, 9 * C)
        first = jnp.dot(both, hi[at, :], preferred_element_type=F32)
        second = jnp.dot(w_hi, lo[at, :], preferred_element_type=F32)
        value = first[:C] + first[C:] + second
        if not is_grad:
            value = value + bias[...]
        result[pl.ds(r, C, stride=R), :] = value[:, :L]
        result[pl.ds(r + half, C, stride=R), :] = value[:, L:]
    token[...] = jnp.zeros((8, L), F32)


def conv(is_grad, *args, after=()):
    blocks = 3 + R // 2 + 3 if is_grad else R // 2 + 2
    scratch = pltpu.VMEM((blocks * 3 * C, 2 * L), BF16)
    return call(
        functools.partial(conv_kernel, is_grad),
        [out(C * R, L), out(8, L)],
        args,
        [scratch, scratch, pltpu.VMEM((2, 1, 2 * L), F32), pltpu.SemaphoreType.DMA((2,))],
        after,
        specs=[VMEM] * (len(args) - 1) + [ANY],
        flops=4 * 6 * 9 * C * C * R * L,
        moved=3 * 4 * C * R * L,
    )


def shards(nlat, nlon, factor, x, weight, bias, g):
    x = x.reshape(C * R, L)
    g = g.reshape(C * R, L)

    def pairs_of(partner):
        pairs = []
        for i in range(nlat):
            for j in range(nlon):
                to_lat, to_lon = partner(i, j)
                pairs.append((i * nlon + j, to_lat * nlon + to_lon))
        return pairs

    def across_2(i, j):
        to = i + 1 if i % 2 else i - 1
        return (to, j) if 0 <= to < nlat else (i, (j + nlon // 2) % nlon)

    to_west = pairs_of(lambda i, j: (i, (j - 1) % nlon))
    to_east = pairs_of(lambda i, j: (i, (j + 1) % nlon))
    first = pairs_of(lambda i, j: (i ^ 1, j))
    second = pairs_of(across_2)

    def send(value, pairs):
        return lax.ppermute(value, AXES, pairs)

    block = 4 * C * R * L
    product = 6 * 9 * C * C * R * L
    own_1, own_2, own_west, own_east, x, g = call(
        front_kernel,
        [kept(2, C, L)] * 2 + [kept(C, L)] * 2 + [kept(C * R, L)] * 2,
        (in_hbm(x), in_hbm(g)),
        [pltpu.SemaphoreType.DMA((PIECES, 2))],
        specs=[ANY] * 2,
        flops=block,
        moved=2 * block,
    )
    row_2 = send(own_2, second)
    row_1 = send(own_1, first)
    east = send(own_west, to_west)
    inner = call(
        inner_weight_kernel,
        [out(C, 7 * L)],
        (x, g),
        [pltpu.VMEM((6 * C, R * L), BF16)] + [pltpu.VMEM((3 * C, R * L), BF16)] * 2,
        flops=product,
        moved=2 * block,
    )[0]

    n_far = lax.axis_size(FAR)
    n_near = nlat * nlon // n_far
    chunks = Chunks(n_near)
    packed = call(
        functools.partial(outer_weight_kernel, chunks),
        [out(n_near * chunks.sent, L)],
        (inner, own_east, own_1, own_2, east, row_1, row_2),
        [pltpu.VMEM((3 * C, 4 * L), BF16)] * 4,
        flops=product // 4,
        moved=block,
    )[0]
    parts = lax.all_to_all(packed.reshape(n_near, 1, chunks.sent * L), NEAR, 0, 0)
    column = call(column_kernel, [kept(C, L)], (own_east, row_1, row_2), after=(packed,))[0]
    west = send(column, to_east)
    mine = call(
        functools.partial(sum_kernel, chunks.rows, chunks.sent),
        [out(n_far * chunks.rows, L)],
        (parts.reshape(n_near * chunks.sent, L),),
        after=(column,),
        moved=block // 2,
    )[0]
    others = lax.all_to_all(mine.reshape(n_far, 1, chunks.rows * L), FAR, 0, 0)
    flipped = weight.reshape(C, 3, 3, C)[:, ::-1, ::-1].transpose(3, 1, 2, 0).reshape(C, 9 * C)
    halo = (west, east, row_1, row_2)
    bias = bias.reshape(C, 1)
    output, token = conv(False, x, *halo, weight, bias, parts)
    mine = call(
        functools.partial(sum_kernel, chunks.rows, chunks.rows),
        [out(n_near * chunks.rows, L)],
        (others.reshape(n_far * chunks.rows, L),),
        after=(token,),
        moved=block // 2,
    )[0]
    gathered = lax.all_to_all(mine.reshape(n_near, 1, chunks.rows * L), NEAR, 0, 0)
    grad, _ = conv(True, g, *halo, flipped, bias, parts, after=(mine,))
    weight_grad, bias_grad = call(
        functools.partial(unpack_kernel, chunks, factor),
        [out(C, 9 * C), out(1, C)],
        (gathered.reshape(n_near * chunks.rows, L),),
        moved=block,
    )
    return (
        output.reshape(C, R, L),
        grad.reshape(C, R, L),
        weight_grad,
        bias_grad.reshape(C),
    )


def solution(mesh):
    nlat, nlon = mesh.shape["lat"], mesh.shape["lon"]
    fine = Mesh(mesh.devices.reshape(nlat, 2, nlon // 8, 2, 2), AXES)
    factor = 1.0 / math.sqrt(nlat * R * nlon * L)
    field = P(None, "lat", LON)
    return jax.shard_map(
        functools.partial(shards, nlat, nlon, factor),
        mesh=fine,
        in_specs=(field, P(), P(), field),
        out_specs=(field, field, P(), P()),
        check_vma=False,
    )
```

```python
import functools
import math

import jax
import jax.numpy as jnp
from jax import lax
from jax.experimental import pallas as pl
from jax.experimental.pallas import tpu as pltpu
from jax.sharding import Mesh
from jax.sharding import PartitionSpec as P

F32 = jnp.float32
BF16 = jnp.bfloat16
C = 96
R = 16
L = 128
HALF = L // 2
NT = (((1,), (1,)), ((), ()))

AXES = ("lat", "xh", "zr", "zd", "c")
LON = ("xh", "zr", "zd", "c")
NEAR = ("lat", "xh", "zd", "c")
FAR = ("zr",)

VMEM = pl.BlockSpec(memory_space=pltpu.VMEM)
ANY = pl.BlockSpec(memory_space=pl.ANY)


def call(kernel, outs, args, scratch=(), after=(), specs=None, grant=40 << 20, flops=0, moved=0):
    def body(*refs):
        kernel(*refs[: len(args)], *refs[len(args) + len(after) :])

    return pl.pallas_call(
        body,
        out_shape=outs,
        in_specs=(specs or [VMEM] * len(args)) + [ANY] * len(after),
        out_specs=[VMEM] * len(outs),
        scratch_shapes=list(scratch),
        compiler_params=pltpu.CompilerParams(vmem_limit_bytes=grant),
        cost_estimate=pl.CostEstimate(flops=flops, bytes_accessed=moved, transcendentals=0),
    )(*args, *after)


def out(*shape):
    return jax.ShapeDtypeStruct(shape, F32)


def kept(*shape):
    return pltpu.VMEM(shape, F32)


def in_hbm(value):
    return pltpu.with_memory_space_constraint(value, pltpu.HBM)


def roll(value, by):
    by = by % L
    return value if by == 0 else pltpu.roll(value, by, 1)


def lanes():
    return lax.broadcasted_iota(jnp.int32, (C, L), 1)


def row(ref, r):
    return ref[pl.ds(r, C, stride=R), :]


def pick(flag, when_set, otherwise):
    return jnp.where(flag == 1, when_set, otherwise)


def split(value):
    high = value.astype(BF16)
    return high, (value - high.astype(F32)).astype(BF16)


def odd_lat():
    return lax.axis_index("lat") % 2


def at_end(place):
    return jnp.where(lax.axis_index("lat") == place, 1.0, 0.0)


def place_of(to):
    nlat = lax.axis_size("lat")
    half = lax.axis_index("xh")
    outside = jnp.logical_or(to < 0, to >= nlat)
    lat = jnp.clip(to, 0, nlat - 1)
    half = jnp.where(outside, 1 - half, half)
    return ((lat * 2 + half) * 2 + lax.axis_index("zd")) * 2 + lax.axis_index("c")


def lat_neighbours():
    lat = lax.axis_index("lat")
    return place_of(lat - 1), place_of(lat + 1)


TILES = 7 * C // 8


class Chunks:
    def __init__(self, n):
        self.n = n
        self.full = 8 * TILES // n
        self.rows = self.full + 1
        self.sent = self.full + 2
        self.halves = 8 * TILES - self.full * n
        assert self.halves in (0, n // 2) and self.full * n % 8 == 0

    def pieces(self, tile):
        at, end = 8 * tile, 8 * tile + 8
        while at < end:
            now = min(self.full - at % self.full, end - at)
            yield at // self.full, at % self.full, now
            at += now


PIECES = 1


def front_kernel(x, g, own_1, own_2, west, east, x_here, g_here, sems):
    step = C // PIECES
    copies = {}
    for k in range(PIECES):
        at = pl.ds(k * step * R, step * R)
        for part, (source, here) in enumerate(((x, x_here), (g, g_here))):
            copies[k, part] = pltpu.make_async_copy(source.at[at, :], here.at[at, :], sems.at[k, part])
            copies[k, part].start()
    odd = odd_lat()
    lane = lax.broadcasted_iota(jnp.int32, (step, L), 1)
    for k in range(PIECES):
        to = pl.ds(k * step, step)
        first = jnp.zeros((step, L), F32)
        last = jnp.zeros((step, L), F32)
        for part, here in enumerate((x_here, g_here)):
            copies[k, part].wait()
            base = HALF * part
            for r in range(R):
                value = here[pl.ds(k * step * R + r, step, stride=R), :]
                if r == 0:
                    top = value
                moved = roll(value, base + r + 1)
                last = jnp.where(lane == base + r, moved, last)
                first = jnp.where(lane == base + r + 1, moved, first)
            own_1[part, to, :] = pick(odd, top, value)
            own_2[part, to, :] = pick(odd, value, top)
        west[to, :] = roll(first, -1)
        east[to, :] = roll(last, 1)


def whole_column(east, row_1, row_2):
    lane = lanes()
    column = east[...]
    odd = odd_lat()
    for part in range(2):
        north = pick(odd, row_1[part], row_2[part])
        south = pick(odd, row_2[part], row_1[part])
        column = jnp.where(lane == HALF * part, roll(north, 1 + HALF * part), column)
        column = jnp.where(lane == HALF * part + R + 1, roll(south, HALF * part + R + 2), column)
    return column


def column_kernel(east, row_1, row_2, column):
    column[...] = whole_column(east, row_1, row_2)


def taps(value, west, west_lane, east, east_lane):
    lane = lanes()
    before = jnp.where(lane == 0, roll(west, -west_lane), roll(value, 1))
    after = jnp.where(lane == L - 1, roll(east, L - 1 - east_lane), roll(value, -1))
    return before, value, after


def nt(left, right):
    return lax.dot_general(left[...], right[...], NT, preferred_element_type=F32)


def wide_form(grad, bias):
    return jnp.concatenate(
        [grad[a * C : (a + 1) * C] for a in range(3)]
        + [bias, jnp.zeros((C, 7 * L - 9 * C - bias.shape[1]), F32)],
        axis=1,
    )


def inner_taps(value):
    lane = lanes()
    before = jnp.where(lane == 0, 0.0, roll(value, 1))
    after = jnp.where(lane == L - 1, 0.0, roll(value, -1))
    return before, value, after


def inner_weight_kernel(x, g, inner, s_both, c_hi, c_lo):
    zero = jnp.zeros((C, L), F32)
    total = zero
    for a, to in ((0, R - 1), (2, 0)):
        c_hi[pl.ds(a * C, C), pl.ds(to * L, L)] = zero.astype(BF16)
        c_lo[pl.ds(a * C, C), pl.ds(to * L, L)] = zero.astype(BF16)
    for r in range(R):
        at = pl.ds(r * L, L)
        for b, shifted in enumerate(inner_taps(row(x, r))):
            s_both[pl.ds(b * C, C), at], s_both[pl.ds((3 + b) * C, C), at] = split(shifted)
        value = row(g, r)
        total = total + value
        high, low = split(value)
        for a in range(3):
            to = r + a - 1
            if 0 <= to < R:
                c_hi[pl.ds(a * C, C), pl.ds(to * L, L)] = high
                c_lo[pl.ds(a * C, C), pl.ds(to * L, L)] = low
    both = nt(c_hi, s_both)
    grad = both[:, : 3 * C] + both[:, 3 * C :] + nt(c_lo, s_both.at[pl.ds(0, 3 * C), :])
    inner[...] = wide_form(grad, jnp.sum(total, axis=1, keepdims=True))


def outer_weight_kernel(
    chunks, inner, own_east, own_1, own_2, east, row_1, row_2, packed, s_both, c_hi, c_lo
):
    lane = lanes()
    zero = jnp.zeros((C, L), F32)
    odd = odd_lat()
    north = pick(odd, row_1[1], row_2[1])
    south = pick(odd, row_2[1], row_1[1])
    x_top = pick(odd, own_1[0], own_2[0])
    x_bottom = pick(odd, own_2[0], own_1[0])
    column = whole_column(own_east, row_1, row_2)
    beyond = east[...]
    at_top = at_end(0)
    at_bottom = at_end(lax.axis_size("lat") - 1)

    def put(k, left, right):
        at = pl.ds(k * L, L)
        for part, value in enumerate(left):
            if value is None:
                c_hi[pl.ds(part * C, C), at] = c_lo[pl.ds(part * C, C), at] = jnp.zeros((C, L), BF16)
            else:
                c_hi[pl.ds(part * C, C), at], c_lo[pl.ds(part * C, C), at] = split(value)
        for part, value in enumerate(right):
            high = pl.ds(part * C, C)
            low = pl.ds((3 + part) * C, C)
            if value is None:
                s_both[high, at] = s_both[low, at] = jnp.zeros((C, L), BF16)
            else:
                s_both[high, at], s_both[low, at] = split(value)

    put(0, (north * at_top, None, north * (1.0 - at_top)), inner_taps(x_top))
    put(1, (south * (1.0 - at_bottom), None, south * at_bottom), inner_taps(x_bottom))
    g_column = roll(column, -HALF)
    below = roll(g_column, -2)
    above = g_column
    south_end = jnp.where(lane == R - 1, below * at_bottom, 0.0)
    north_end = jnp.where(lane == 0, above * at_top, 0.0)
    shifted = (below - south_end + north_end, roll(g_column, -1), above - north_end + south_end)
    left = []
    for a, value in enumerate(shifted):
        other = jnp.where(lane < HALF + a + R, roll(beyond, a), 0.0)
        left.append(jnp.where(lane < HALF, value, jnp.where(lane < HALF + a, 0.0, other)))
    own = jnp.where(lane < HALF + R + 2, roll(column, HALF), 0.0)
    put(2, left, (jnp.where(lane < HALF, 0.0, own), None, jnp.where(lane < R, beyond, 0.0)))
    both = nt(c_hi, s_both)
    grad = both[:, : 3 * C] + both[:, 3 * C :] + nt(c_lo, s_both.at[pl.ds(0, 3 * C), :])
    wide = inner[...] + wide_form(grad, jnp.zeros((C, 1), F32))
    cells = zero
    for k, at in enumerate((0, HALF, R - 1, HALF + R - 1)):
        cells = jnp.where(lane == k, roll(beyond, k - at), cells)
    cells = jnp.concatenate([cells, jnp.zeros((L - C, L), F32)], axis=0).T
    x_cells = roll(cells[0:8], HALF)
    g_cells = roll(cells[0:8], L // 4)
    lane = lax.broadcasted_iota(jnp.int32, (1, L), 1)
    corners = []
    for k in (0, 2):
        moved = x_cells[k : k + 1]
        corners.append((moved, jnp.where(lane < L // 4, moved, g_cells[k + 1 : k + 2])))
    to_north, to_south = lat_neighbours()
    left = chunks.full * chunks.n // 8
    for tile in range(TILES):
        i, j = divmod(tile, 7)
        value = wide[8 * i : 8 * i + 8, L * j : L * j + L]
        if tile < left:
            at = 0
            for chunk, place, count in chunks.pieces(tile):
                packed[pl.ds(chunk * chunks.sent + place, count), :] = value[at : at + count]
                at += count
        else:
            for k, half in enumerate((value, roll(value, HALF))):
                for r in range(8):
                    chunk = 2 * (8 * (tile - left) + r) + k
                    packed[pl.ds(chunk * chunks.sent + chunks.full, 1), :] = half[r : r + 1]
    for chunk in range(chunks.n):
        at = chunk * chunks.sent + chunks.full
        first = jnp.where(to_north == chunk, corners[0][0], jnp.where(to_south == chunk, corners[1][0], 0.0))
        if chunks.halves:
            first = jnp.where(lane < HALF, packed[pl.ds(at, 1), :], first)
        packed[pl.ds(at, 1), :] = first
        packed[pl.ds(at + 1, 1), :] = jnp.where(
            to_north == chunk, corners[0][1], jnp.where(to_south == chunk, corners[1][1], 0.0)
        )


def sum_kernel(rows, height, parts, result):
    total = parts[pl.ds(0, rows), :]
    for k in range(1, parts.shape[0] // height):
        total = total + parts[pl.ds(k * height, rows), :]
    for k in range(result.shape[0] // rows):
        result[pl.ds(k * rows, rows), :] = total


def unpack_kernel(chunks, factor, gathered, weight_grad, bias_grad):
    lane = lax.broadcasted_iota(jnp.int32, (8, L), 1)
    left = chunks.full * chunks.n // 8
    ends = []
    for tile in range(TILES):
        i, j = divmod(tile, 7)
        if tile < left:
            value = jnp.concatenate(
                [
                    gathered[pl.ds(chunk * chunks.rows + place, count), :]
                    for chunk, place, count in chunks.pieces(tile)
                ],
                axis=0,
            )
        else:
            at = 16 * (tile - left) * chunks.rows + chunks.full
            even, odd = (
                gathered[pl.ds(at + k * chunks.rows, 8, stride=2 * chunks.rows), :] for k in range(2)
            )
            value = jnp.where(lane < HALF, even, roll(odd, HALF))
        width = min(L, 9 * C - L * j)
        weight_grad[pl.ds(8 * i, 8), pl.ds(L * j, width)] = value[:, :width] * factor
        if width < L:
            ends.append(value)
    ends = jnp.concatenate(ends + [jnp.zeros((L - C, L), F32)], axis=0).T
    at = 9 * C % L
    bias_grad[...] = ends[at : at + 1, :C] * factor


def conv_kernel(
    is_grad, field, west, east, row_1, row_2, weight, bias, parts, result, token, hi, lo, ends, sems
):
    part = 1 if is_grad else 0
    copies = [
        pltpu.make_async_copy(
            parts.at[at, :, pl.ds(parts.shape[2] - 2 * L, 2 * L)], ends.at[k], sems.at[k]
        )
        for k, at in enumerate(lat_neighbours())
    ]
    for copy in copies:
        copy.start()
    odd = odd_lat()
    north = pick(odd, row_1[part], row_2[part])
    south = pick(odd, row_2[part], row_1[part])
    for copy in copies:
        copy.wait()
    lane = lax.broadcasted_iota(jnp.int32, (1, L), 1)
    corners = []
    for k in range(2):
        former, latter = ends[k][:, :L], ends[k][:, L:]
        if is_grad:
            corners.append(roll(latter, -(L // 4)))
        else:
            corners.append(jnp.where(lane < HALF, roll(former, HALF), roll(latter, HALF)))
    corners = jnp.concatenate(corners + [jnp.zeros((L - 2, L), F32)], axis=0).T[:C]
    first = HALF * part

    def shifts(r):
        if r < 0:
            return taps(north, west[...], first + r + 1, corners, 0)
        if r >= R:
            return taps(south, west[...], first + r + 1, corners, 1)
        return taps(row(field, r), west[...], first + r + 1, east[...], first + r)

    def put(block, half, values):
        for b, value in enumerate(values):
            at = (pl.ds((3 * block + b) * C, C), pl.ds(half * L, L))
            hi[at], lo[at] = split(value)

    half = R // 2
    if is_grad:
        at_top = at_end(0)
        at_bottom = at_end(lax.axis_size("lat") - 1)
        outer_top = shifts(-1)
        outer_bottom = shifts(R)
        put(0, 0, [v * (1.0 - at_top) for v in outer_top])
        put(0, 1, shifts(half - 1))
        put(1, 0, shifts(0))
        put(1, 1, shifts(half))
        put(2, 0, [v + o * at_top for v, o in zip(shifts(1), outer_top)])
        put(2, 1, shifts(half + 1))
        for r in range(half):
            put(3 + r, 0, shifts(r))
            put(3 + r, 1, shifts(r + half))
        k = 3 + half
        put(k, 0, shifts(half - 2))
        put(k, 1, [v + o * at_bottom for v, o in zip(shifts(R - 2), outer_bottom)])
        put(k + 1, 0, shifts(half - 1))
        put(k + 1, 1, shifts(R - 1))
        put(k + 2, 0, shifts(half))
        put(k + 2, 1, [v * (1.0 - at_bottom) for v in outer_bottom])
        starts = [0] + [2 + r for r in range(1, half - 1)] + [k]
    else:
        for j in range(half + 2):
            put(j, 0, shifts(j - 1))
            put(j, 1, shifts(j - 1 + half))
        starts = list(range(half))
    w_hi, w_lo = split(weight[...])
    both = jnp.concatenate([w_hi, w_lo], axis=0)
    for r, start in enumerate(starts):
        at = pl.ds(start * 3 * C, 9 * C)
        first = jnp.dot(both, hi[at, :], preferred_element_type=F32)
        second = jnp.dot(w_hi, lo[at, :], preferred_element_type=F32)
        value = first[:C] + first[C:] + second
        if not is_grad:
            value = value + bias[...]
        result[pl.ds(r, C, stride=R), :] = value[:, :L]
        result[pl.ds(r + half, C, stride=R), :] = value[:, L:]
    token[...] = jnp.zeros((8, L), F32)


def conv(is_grad, *args, after=()):
    blocks = 3 + R // 2 + 3 if is_grad else R // 2 + 2
    scratch = pltpu.VMEM((blocks * 3 * C, 2 * L), BF16)
    return call(
        functools.partial(conv_kernel, is_grad),
        [out(C * R, L), out(8, L)],
        args,
        [scratch, scratch, pltpu.VMEM((2, 1, 2 * L), F32), pltpu.SemaphoreType.DMA((2,))],
        after,
        specs=[VMEM] * (len(args) - 1) + [ANY],
        flops=4 * 6 * 9 * C * C * R * L,
        moved=3 * 4 * C * R * L,
    )


def shards(nlat, nlon, factor, x, weight, bias, g):
    x = x.reshape(C * R, L)
    g = g.reshape(C * R, L)

    def pairs_of(partner):
        pairs = []
        for i in range(nlat):
            for j in range(nlon):
                to_lat, to_lon = partner(i, j)
                pairs.append((i * nlon + j, to_lat * nlon + to_lon))
        return pairs

    def across_2(i, j):
        to = i + 1 if i % 2 else i - 1
        return (to, j) if 0 <= to < nlat else (i, (j + nlon // 2) % nlon)

    to_west = pairs_of(lambda i, j: (i, (j - 1) % nlon))
    to_east = pairs_of(lambda i, j: (i, (j + 1) % nlon))
    first = pairs_of(lambda i, j: (i ^ 1, j))
    second = pairs_of(across_2)

    def send(value, pairs):
        return lax.ppermute(value, AXES, pairs)

    block = 4 * C * R * L
    product = 6 * 9 * C * C * R * L
    own_1, own_2, own_west, own_east, x, g = call(
        front_kernel,
        [kept(2, C, L)] * 2 + [kept(C, L)] * 2 + [kept(C * R, L)] * 2,
        (in_hbm(x), in_hbm(g)),
        [pltpu.SemaphoreType.DMA((PIECES, 2))],
        specs=[ANY] * 2,
        flops=block,
        moved=2 * block,
    )
    row_2 = send(own_2, second)
    row_1 = send(own_1, first)
    east = send(own_west, to_west)
    inner = call(
        inner_weight_kernel,
        [out(C, 7 * L)],
        (x, g),
        [pltpu.VMEM((6 * C, R * L), BF16)] + [pltpu.VMEM((3 * C, R * L), BF16)] * 2,
        flops=product,
        moved=2 * block,
    )[0]

    n_far = lax.axis_size(FAR)
    n_near = nlat * nlon // n_far
    chunks = Chunks(n_near)
    packed = call(
        functools.partial(outer_weight_kernel, chunks),
        [out(n_near * chunks.sent, L)],
        (inner, own_east, own_1, own_2, east, row_1, row_2),
        [pltpu.VMEM((6 * C, 3 * L), BF16)] + [pltpu.VMEM((3 * C, 3 * L), BF16)] * 2,
        flops=product // 4,
        moved=block,
    )[0]
    parts = lax.all_to_all(packed.reshape(n_near, 1, chunks.sent * L), NEAR, 0, 0)
    column = call(column_kernel, [kept(C, L)], (own_east, row_1, row_2), after=(packed,))[0]
    west = send(column, to_east)
    mine = call(
        functools.partial(sum_kernel, chunks.rows, chunks.sent),
        [out(n_far * chunks.rows, L)],
        (parts.reshape(n_near * chunks.sent, L),),
        after=(column,),
        moved=block // 2,
    )[0]
    others = lax.all_to_all(mine.reshape(n_far, 1, chunks.rows * L), FAR, 0, 0)
    flipped = weight.reshape(C, 3, 3, C)[:, ::-1, ::-1].transpose(3, 1, 2, 0).reshape(C, 9 * C)
    halo = (west, east, row_1, row_2)
    bias = bias.reshape(C, 1)
    output, token = conv(False, x, *halo, weight, bias, parts)
    mine = call(
        functools.partial(sum_kernel, chunks.rows, chunks.rows),
        [out(n_near * chunks.rows, L)],
        (others.reshape(n_far * chunks.rows, L),),
        after=(token,),
        moved=block // 2,
    )[0]
    gathered = lax.all_to_all(mine.reshape(n_near, 1, chunks.rows * L), NEAR, 0, 0)
    grad, _ = conv(True, g, *halo, flipped, bias, parts, after=(mine,))
    weight_grad, bias_grad = call(
        functools.partial(unpack_kernel, chunks, factor),
        [out(C, 9 * C), out(1, C)],
        (gathered.reshape(n_near * chunks.rows, L),),
        moved=block,
    )
    return (
        output.reshape(C, R, L),
        grad.reshape(C, R, L),
        weight_grad,
        bias_grad.reshape(C),
    )


def solution(mesh):
    nlat, nlon = mesh.shape["lat"], mesh.shape["lon"]
    fine = Mesh(mesh.devices.reshape(nlat, 2, nlon // 8, 2, 2), AXES)
    factor = 1.0 / math.sqrt(nlat * R * nlon * L)
    field = P(None, "lat", LON)
    return jax.shard_map(
        functools.partial(shards, nlat, nlon, factor),
        mesh=fine,
        in_specs=(field, P(), P(), field),
        out_specs=(field, field, P(), P()),
        check_vma=False,
    )
```

```python
import functools
import math

import jax
import jax.numpy as jnp
from jax import lax
from jax.experimental import pallas as pl
from jax.experimental.pallas import tpu as pltpu
from jax.sharding import Mesh
from jax.sharding import PartitionSpec as P

F32 = jnp.float32
BF16 = jnp.bfloat16
C = 96
R = 16
L = 128
HALF = L // 2
NT = (((1,), (1,)), ((), ()))

AXES = ("lat", "xh", "zr", "zd", "c")
LON = ("xh", "zr", "zd", "c")
NEAR = ("lat", "xh", "zd", "c")
FAR = ("zr",)

VMEM = pl.BlockSpec(memory_space=pltpu.VMEM)
ANY = pl.BlockSpec(memory_space=pl.ANY)


def call(kernel, outs, args, scratch=(), after=(), specs=None, grant=40 << 20, flops=0, moved=0):
    def body(*refs):
        kernel(*refs[: len(args)], *refs[len(args) + len(after) :])

    return pl.pallas_call(
        body,
        out_shape=outs,
        in_specs=(specs or [VMEM] * len(args)) + [ANY] * len(after),
        out_specs=[VMEM] * len(outs),
        scratch_shapes=list(scratch),
        compiler_params=pltpu.CompilerParams(vmem_limit_bytes=grant),
        cost_estimate=pl.CostEstimate(flops=flops, bytes_accessed=moved, transcendentals=0),
    )(*args, *after)


def out(*shape):
    return jax.ShapeDtypeStruct(shape, F32)


def kept(*shape):
    return pltpu.VMEM(shape, F32)


def in_hbm(value):
    return pltpu.with_memory_space_constraint(value, pltpu.HBM)


def roll(value, by):
    by = by % L
    return value if by == 0 else pltpu.roll(value, by, 1)


def lanes():
    return lax.broadcasted_iota(jnp.int32, (C, L), 1)


def row(ref, r):
    return ref[pl.ds(r, C, stride=R), :]


def pick(flag, when_set, otherwise):
    return jnp.where(flag == 1, when_set, otherwise)


def split(value):
    high = value.astype(BF16)
    return high, (value - high.astype(F32)).astype(BF16)


def odd_lat():
    return lax.axis_index("lat") % 2


def at_end(place):
    return jnp.where(lax.axis_index("lat") == place, 1.0, 0.0)


def place_of(to):
    nlat = lax.axis_size("lat")
    half = lax.axis_index("xh")
    outside = jnp.logical_or(to < 0, to >= nlat)
    lat = jnp.clip(to, 0, nlat - 1)
    half = jnp.where(outside, 1 - half, half)
    return ((lat * 2 + half) * 2 + lax.axis_index("zd")) * 2 + lax.axis_index("c")


def lat_neighbours():
    lat = lax.axis_index("lat")
    return place_of(lat - 1), place_of(lat + 1)


TILES = 7 * C // 8


class Chunks:
    def __init__(self, n):
        self.n = n
        self.full = 8 * TILES // n
        self.rows = self.full + 1
        self.sent = self.full + 2
        self.halves = 8 * TILES - self.full * n
        assert self.halves in (0, n // 2) and self.full * n % 8 == 0

    def pieces(self, tile):
        at, end = 8 * tile, 8 * tile + 8
        while at < end:
            now = min(self.full - at % self.full, end - at)
            yield at // self.full, at % self.full, now
            at += now


PIECES = 1


def front_kernel(x, g, own_1, own_2, west, east, x_here, g_here, sems):
    step = C // PIECES
    copies = {}
    for k in range(PIECES):
        at = pl.ds(k * step * R, step * R)
        for part, (source, here) in enumerate(((x, x_here), (g, g_here))):
            copies[k, part] = pltpu.make_async_copy(source.at[at, :], here.at[at, :], sems.at[k, part])
            copies[k, part].start()
    odd = odd_lat()
    lane = lax.broadcasted_iota(jnp.int32, (step, L), 1)
    for k in range(PIECES):
        to = pl.ds(k * step, step)
        first = jnp.zeros((step, L), F32)
        last = jnp.zeros((step, L), F32)
        for part, here in enumerate((x_here, g_here)):
            copies[k, part].wait()
            base = HALF * part
            for r in range(R):
                value = here[pl.ds(k * step * R + r, step, stride=R), :]
                if r == 0:
                    top = value
                moved = roll(value, base + r + 1)
                last = jnp.where(lane == base + r, moved, last)
                first = jnp.where(lane == base + r + 1, moved, first)
            own_1[part, to, :] = pick(odd, top, value)
            own_2[part, to, :] = pick(odd, value, top)
        west[to, :] = roll(first, -1)
        east[to, :] = roll(last, 1)


def whole_column(east, row_1, row_2):
    lane = lanes()
    column = east[...]
    odd = odd_lat()
    for part in range(2):
        north = pick(odd, row_1[part], row_2[part])
        south = pick(odd, row_2[part], row_1[part])
        column = jnp.where(lane == HALF * part, roll(north, 1 + HALF * part), column)
        column = jnp.where(lane == HALF * part + R + 1, roll(south, HALF * part + R + 2), column)
    return column


def column_kernel(east, row_1, row_2, column):
    column[...] = whole_column(east, row_1, row_2)


def taps(value, west, west_lane, east, east_lane):
    lane = lanes()
    before = jnp.where(lane == 0, roll(west, -west_lane), roll(value, 1))
    after = jnp.where(lane == L - 1, roll(east, L - 1 - east_lane), roll(value, -1))
    return before, value, after


def nt(left, right):
    return lax.dot_general(left[...], right[...], NT, preferred_element_type=F32)


def wide_form(grad, bias):
    return jnp.concatenate(
        [grad[a * C : (a + 1) * C] for a in range(3)]
        + [bias, jnp.zeros((C, 7 * L - 9 * C - bias.shape[1]), F32)],
        axis=1,
    )


def inner_taps(value):
    lane = lanes()
    before = jnp.where(lane == 0, 0.0, roll(value, 1))
    after = jnp.where(lane == L - 1, 0.0, roll(value, -1))
    return before, value, after


def inner_weight_kernel(x, g, inner, s_both, c_hi, c_lo):
    zero = jnp.zeros((C, L), F32)
    total = zero
    for a, to in ((0, R - 1), (2, 0)):
        c_hi[pl.ds(a * C, C), pl.ds(to * L, L)] = zero.astype(BF16)
        c_lo[pl.ds(a * C, C), pl.ds(to * L, L)] = zero.astype(BF16)
    for r in range(R):
        at = pl.ds(r * L, L)
        for b, shifted in enumerate(inner_taps(row(x, r))):
            s_both[pl.ds(b * C, C), at], s_both[pl.ds((3 + b) * C, C), at] = split(shifted)
        value = row(g, r)
        total = total + value
        high, low = split(value)
        for a in range(3):
            to = r + a - 1
            if 0 <= to < R:
                c_hi[pl.ds(a * C, C), pl.ds(to * L, L)] = high
                c_lo[pl.ds(a * C, C), pl.ds(to * L, L)] = low
    both = nt(c_hi, s_both)
    grad = both[:, : 3 * C] + both[:, 3 * C :] + nt(c_lo, s_both.at[pl.ds(0, 3 * C), :])
    inner[...] = wide_form(grad, jnp.sum(total, axis=1, keepdims=True))


def outer_weight_kernel(
    chunks, inner, own_east, own_1, own_2, east, row_1, row_2, packed, s_both, c_hi, c_lo
):
    lane = lanes()
    zero = jnp.zeros((C, L), F32)
    odd = odd_lat()
    north = pick(odd, row_1[1], row_2[1])
    south = pick(odd, row_2[1], row_1[1])
    x_top = pick(odd, own_1[0], own_2[0])
    x_bottom = pick(odd, own_2[0], own_1[0])
    column = whole_column(own_east, row_1, row_2)
    beyond = east[...]
    at_top = at_end(0)
    at_bottom = at_end(lax.axis_size("lat") - 1)

    def put(k, left, right):
        at = pl.ds(k * L, L)
        for part, value in enumerate(left):
            if value is None:
                c_hi[pl.ds(part * C, C), at] = c_lo[pl.ds(part * C, C), at] = jnp.zeros((C, L), BF16)
            else:
                c_hi[pl.ds(part * C, C), at], c_lo[pl.ds(part * C, C), at] = split(value)
        for part, value in enumerate(right):
            high = pl.ds(part * C, C)
            low = pl.ds((3 + part) * C, C)
            if value is None:
                s_both[high, at] = s_both[low, at] = jnp.zeros((C, L), BF16)
            else:
                s_both[high, at], s_both[low, at] = split(value)

    put(0, (north * at_top, None, north * (1.0 - at_top)), inner_taps(x_top))
    put(1, (south * (1.0 - at_bottom), None, south * at_bottom), inner_taps(x_bottom))
    g_column = roll(column, -HALF)
    below = roll(g_column, -2)
    above = g_column
    south_end = jnp.where(lane == R - 1, below * at_bottom, 0.0)
    north_end = jnp.where(lane == 0, above * at_top, 0.0)
    shifted = (below - south_end + north_end, roll(g_column, -1), above - north_end + south_end)
    left = []
    for a, value in enumerate(shifted):
        other = jnp.where(lane < HALF + a + R, roll(beyond, a), 0.0)
        left.append(jnp.where(lane < HALF, value, jnp.where(lane < HALF + a, 0.0, other)))
    own = jnp.where(lane < HALF + R + 2, roll(column, HALF), 0.0)
    put(2, left, (jnp.where(lane < HALF, 0.0, own), None, jnp.where(lane < R, beyond, 0.0)))
    both = nt(c_hi, s_both)
    grad = both[:, : 3 * C] + both[:, 3 * C :] + nt(c_lo, s_both.at[pl.ds(0, 3 * C), :])
    wide = inner[...] + wide_form(grad, jnp.zeros((C, 1), F32))
    cells = zero
    for k, at in enumerate((0, HALF, R - 1, HALF + R - 1)):
        cells = jnp.where(lane == k, roll(beyond, k - at), cells)
    cells = jnp.concatenate([cells, jnp.zeros((L - C, L), F32)], axis=0).T
    x_cells = roll(cells[0:8], HALF)
    g_cells = roll(cells[0:8], L // 4)
    lane = lax.broadcasted_iota(jnp.int32, (1, L), 1)
    corners = []
    for k in (0, 2):
        moved = x_cells[k : k + 1]
        corners.append((moved, jnp.where(lane < L // 4, moved, g_cells[k + 1 : k + 2])))
    to_north, to_south = lat_neighbours()
    left = chunks.full * chunks.n // 8
    for tile in range(TILES):
        i, j = divmod(tile, 7)
        value = wide[8 * i : 8 * i + 8, L * j : L * j + L]
        if tile < left:
            at = 0
            for chunk, place, count in chunks.pieces(tile):
                packed[pl.ds(chunk * chunks.sent + place, count), :] = value[at : at + count]
                at += count
        else:
            for k, half in enumerate((value, roll(value, HALF))):
                for r in range(8):
                    chunk = 2 * (8 * (tile - left) + r) + k
                    packed[pl.ds(chunk * chunks.sent + chunks.full, 1), :] = half[r : r + 1]
    for chunk in range(chunks.n):
        at = chunk * chunks.sent + chunks.full
        first = jnp.where(to_north == chunk, corners[0][0], jnp.where(to_south == chunk, corners[1][0], 0.0))
        if chunks.halves:
            first = jnp.where(lane < HALF, packed[pl.ds(at, 1), :], first)
        packed[pl.ds(at, 1), :] = first
        packed[pl.ds(at + 1, 1), :] = jnp.where(
            to_north == chunk, corners[0][1], jnp.where(to_south == chunk, corners[1][1], 0.0)
        )


def sum_kernel(rows, height, parts, result):
    total = parts[pl.ds(0, rows), :]
    for k in range(1, parts.shape[0] // height):
        total = total + parts[pl.ds(k * height, rows), :]
    for k in range(result.shape[0] // rows):
        result[pl.ds(k * rows, rows), :] = total


def unpack_kernel(chunks, factor, gathered, weight_grad, bias_grad):
    lane = lax.broadcasted_iota(jnp.int32, (8, L), 1)
    left = chunks.full * chunks.n // 8
    ends = []
    for tile in range(TILES):
        i, j = divmod(tile, 7)
        if tile < left:
            value = jnp.concatenate(
                [
                    gathered[pl.ds(chunk * chunks.rows + place, count), :]
                    for chunk, place, count in chunks.pieces(tile)
                ],
                axis=0,
            )
        else:
            at = 16 * (tile - left) * chunks.rows + chunks.full
            even, odd = (
                gathered[pl.ds(at + k * chunks.rows, 8, stride=2 * chunks.rows), :] for k in range(2)
            )
            value = jnp.where(lane < HALF, even, roll(odd, HALF))
        width = min(L, 9 * C - L * j)
        weight_grad[pl.ds(8 * i, 8), pl.ds(L * j, width)] = value[:, :width] * factor
        if width < L:
            ends.append(value)
    ends = jnp.concatenate(ends + [jnp.zeros((L - C, L), F32)], axis=0).T
    at = 9 * C % L
    bias_grad[...] = ends[at : at + 1, :C] * factor


def conv_kernel(
    is_grad, field, west, east, row_1, row_2, weight, bias, parts, result, token, hi, lo, ends, sems
):
    part = 1 if is_grad else 0
    copies = [
        pltpu.make_async_copy(
            parts.at[at, :, pl.ds(parts.shape[2] - 2 * L, 2 * L)], ends.at[k], sems.at[k]
        )
        for k, at in enumerate(lat_neighbours())
    ]
    for copy in copies:
        copy.start()
    odd = odd_lat()
    north = pick(odd, row_1[part], row_2[part])
    south = pick(odd, row_2[part], row_1[part])
    for copy in copies:
        copy.wait()
    lane = lax.broadcasted_iota(jnp.int32, (1, L), 1)
    corners = []
    for k in range(2):
        former, latter = ends[k][:, :L], ends[k][:, L:]
        if is_grad:
            corners.append(roll(latter, -(L // 4)))
        else:
            corners.append(jnp.where(lane < HALF, roll(former, HALF), roll(latter, HALF)))
    corners = jnp.concatenate(corners + [jnp.zeros((L - 2, L), F32)], axis=0).T[:C]
    first = HALF * part

    def shifts(r):
        if r < 0:
            return taps(north, west[...], first + r + 1, corners, 0)
        if r >= R:
            return taps(south, west[...], first + r + 1, corners, 1)
        return taps(row(field, r), west[...], first + r + 1, east[...], first + r)

    def put(block, half, values):
        for b, value in enumerate(values):
            at = (pl.ds((3 * block + b) * C, C), pl.ds(half * L, L))
            hi[at], lo[at] = split(value)

    half = R // 2
    if is_grad:
        at_top = at_end(0)
        at_bottom = at_end(lax.axis_size("lat") - 1)
        outer_top = shifts(-1)
        outer_bottom = shifts(R)
        put(0, 0, [v * (1.0 - at_top) for v in outer_top])
        put(0, 1, shifts(half - 1))
        put(1, 0, shifts(0))
        put(1, 1, shifts(half))
        put(2, 0, [v + o * at_top for v, o in zip(shifts(1), outer_top)])
        put(2, 1, shifts(half + 1))
        for r in range(half):
            put(3 + r, 0, shifts(r))
            put(3 + r, 1, shifts(r + half))
        k = 3 + half
        put(k, 0, shifts(half - 2))
        put(k, 1, [v + o * at_bottom for v, o in zip(shifts(R - 2), outer_bottom)])
        put(k + 1, 0, shifts(half - 1))
        put(k + 1, 1, shifts(R - 1))
        put(k + 2, 0, shifts(half))
        put(k + 2, 1, [v * (1.0 - at_bottom) for v in outer_bottom])
        starts = [0] + [2 + r for r in range(1, half - 1)] + [k]
    else:
        for j in range(half + 2):
            put(j, 0, shifts(j - 1))
            put(j, 1, shifts(j - 1 + half))
        starts = list(range(half))
    w_hi, w_lo = split(weight[...])
    both = jnp.concatenate([w_hi, w_lo], axis=0)
    for r, start in enumerate(starts):
        at = pl.ds(start * 3 * C, 9 * C)
        first = jnp.dot(both, hi[at, :], preferred_element_type=F32)
        second = jnp.dot(w_hi, lo[at, :], preferred_element_type=F32)
        value = first[:C] + first[C:] + second
        if not is_grad:
            value = value + bias[...]
        result[pl.ds(r, C, stride=R), :] = value[:, :L]
        result[pl.ds(r + half, C, stride=R), :] = value[:, L:]
    token[...] = jnp.zeros((8, L), F32)


def conv(is_grad, *args, after=()):
    blocks = 3 + R // 2 + 3 if is_grad else R // 2 + 2
    scratch = pltpu.VMEM((blocks * 3 * C, 2 * L), BF16)
    return call(
        functools.partial(conv_kernel, is_grad),
        [out(C * R, L), out(8, L)],
        args,
        [scratch, scratch, pltpu.VMEM((2, 1, 2 * L), F32), pltpu.SemaphoreType.DMA((2,))],
        after,
        specs=[VMEM] * (len(args) - 1) + [ANY],
        flops=4 * 6 * 9 * C * C * R * L,
        moved=3 * 4 * C * R * L,
    )


def shards(nlat, nlon, factor, x, weight, bias, g):
    x = x.reshape(C * R, L)
    g = g.reshape(C * R, L)

    def pairs_of(partner):
        pairs = []
        for i in range(nlat):
            for j in range(nlon):
                to_lat, to_lon = partner(i, j)
                pairs.append((i * nlon + j, to_lat * nlon + to_lon))
        return pairs

    def across_2(i, j):
        to = i + 1 if i % 2 else i - 1
        return (to, j) if 0 <= to < nlat else (i, (j + nlon // 2) % nlon)

    to_west = pairs_of(lambda i, j: (i, (j - 1) % nlon))
    to_east = pairs_of(lambda i, j: (i, (j + 1) % nlon))
    first = pairs_of(lambda i, j: (i ^ 1, j))
    second = pairs_of(across_2)

    def send(value, pairs):
        return lax.ppermute(value, AXES, pairs)

    block = 4 * C * R * L
    product = 6 * 9 * C * C * R * L
    own_1, own_2, own_west, own_east, x, g = call(
        front_kernel,
        [kept(2, C, L)] * 2 + [kept(C, L)] * 2 + [kept(C * R, L)] * 2,
        (in_hbm(x), in_hbm(g)),
        [pltpu.SemaphoreType.DMA((PIECES, 2))],
        specs=[ANY] * 2,
        flops=block,
        moved=2 * block,
    )
    row_2 = send(own_2, second)
    row_1 = send(own_1, first)
    east = send(own_west, to_west)
    inner = call(
        inner_weight_kernel,
        [out(C, 7 * L)],
        (x, g),
        [pltpu.VMEM((6 * C, R * L), BF16)] + [pltpu.VMEM((3 * C, R * L), BF16)] * 2,
        flops=product,
        moved=2 * block,
    )[0]

    n_far = lax.axis_size(FAR)
    n_near = nlat * nlon // n_far
    chunks = Chunks(n_near)
    packed = call(
        functools.partial(outer_weight_kernel, chunks),
        [out(n_near * chunks.sent, L)],
        (inner, own_east, own_1, own_2, east, row_1, row_2),
        [pltpu.VMEM((6 * C, 3 * L), BF16)] + [pltpu.VMEM((3 * C, 3 * L), BF16)] * 2,
        flops=product // 4,
        moved=block,
    )[0]
    parts = lax.all_to_all(packed.reshape(n_near, 1, chunks.sent * L), NEAR, 0, 0)
    mine = call(
        functools.partial(sum_kernel, chunks.rows, chunks.sent),
        [out(n_far * chunks.rows, L)],
        (parts.reshape(n_near * chunks.sent, L),),
        moved=block // 2,
    )[0]
    column = call(column_kernel, [kept(C, L)], (own_east, row_1, row_2), after=(mine,))[0]
    west = send(column, to_east)
    others = lax.all_to_all(mine.reshape(n_far, 1, chunks.rows * L), FAR, 0, 0)
    flipped = weight.reshape(C, 3, 3, C)[:, ::-1, ::-1].transpose(3, 1, 2, 0).reshape(C, 9 * C)
    halo = (west, east, row_1, row_2)
    bias = bias.reshape(C, 1)
    mine = call(
        functools.partial(sum_kernel, chunks.rows, chunks.rows),
        [out(n_near * chunks.rows, L)],
        (others.reshape(n_far * chunks.rows, L),),
        after=(west, flipped, bias),
        moved=block // 2,
    )[0]
    gathered = lax.all_to_all(mine.reshape(n_near, 1, chunks.rows * L), NEAR, 0, 0)
    output, _ = conv(False, x, *halo, weight, bias, parts, after=(mine,))
    grad, _ = conv(True, g, *halo, flipped, bias, parts, after=(mine,))
    weight_grad, bias_grad = call(
        functools.partial(unpack_kernel, chunks, factor),
        [out(C, 9 * C), out(1, C)],
        (gathered.reshape(n_near * chunks.rows, L),),
        moved=block,
    )
    return (
        output.reshape(C, R, L),
        grad.reshape(C, R, L),
        weight_grad,
        bias_grad.reshape(C),
    )


def solution(mesh):
    nlat, nlon = mesh.shape["lat"], mesh.shape["lon"]
    fine = Mesh(mesh.devices.reshape(nlat, 2, nlon // 8, 2, 2), AXES)
    factor = 1.0 / math.sqrt(nlat * R * nlon * L)
    field = P(None, "lat", LON)
    return jax.shard_map(
        functools.partial(shards, nlat, nlon, factor),
        mesh=fine,
        in_specs=(field, P(), P(), field),
        out_specs=(field, field, P(), P()),
        check_vma=False,
    )
```

```python
import functools
import math

import jax
import jax.numpy as jnp
from jax import lax
from jax.experimental import pallas as pl
from jax.experimental.pallas import tpu as pltpu
from jax.sharding import Mesh
from jax.sharding import PartitionSpec as P

F32 = jnp.float32
BF16 = jnp.bfloat16
C = 96
R = 16
L = 128
HALF = L // 2
NT = (((1,), (1,)), ((), ()))

AXES = ("lat", "xh", "zr", "zd", "c")
LON = ("xh", "zr", "zd", "c")
NEAR = ("lat", "xh", "zd", "c")
FAR = ("zr",)

VMEM = pl.BlockSpec(memory_space=pltpu.VMEM)
ANY = pl.BlockSpec(memory_space=pl.ANY)


def call(kernel, outs, args, scratch=(), after=(), specs=None, grant=40 << 20, flops=0, moved=0):
    def body(*refs):
        kernel(*refs[: len(args)], *refs[len(args) + len(after) :])

    return pl.pallas_call(
        body,
        out_shape=outs,
        in_specs=(specs or [VMEM] * len(args)) + [ANY] * len(after),
        out_specs=[VMEM] * len(outs),
        scratch_shapes=list(scratch),
        compiler_params=pltpu.CompilerParams(vmem_limit_bytes=grant),
        cost_estimate=pl.CostEstimate(flops=flops, bytes_accessed=moved, transcendentals=0),
    )(*args, *after)


def out(*shape):
    return jax.ShapeDtypeStruct(shape, F32)


def kept(*shape):
    return pltpu.VMEM(shape, F32)


def in_hbm(value):
    return pltpu.with_memory_space_constraint(value, pltpu.HBM)


def roll(value, by):
    by = by % L
    return value if by == 0 else pltpu.roll(value, by, 1)


def lanes():
    return lax.broadcasted_iota(jnp.int32, (C, L), 1)


def row(ref, r):
    return ref[pl.ds(r, C, stride=R), :]


def pick(flag, when_set, otherwise):
    return jnp.where(flag == 1, when_set, otherwise)


def split(value):
    high = value.astype(BF16)
    return high, (value - high.astype(F32)).astype(BF16)


def odd_lat():
    return lax.axis_index("lat") % 2


def at_end(place):
    return jnp.where(lax.axis_index("lat") == place, 1.0, 0.0)


def place_of(to):
    nlat = lax.axis_size("lat")
    half = lax.axis_index("xh")
    outside = jnp.logical_or(to < 0, to >= nlat)
    lat = jnp.clip(to, 0, nlat - 1)
    half = jnp.where(outside, 1 - half, half)
    return ((lat * 2 + half) * 2 + lax.axis_index("zd")) * 2 + lax.axis_index("c")


def lat_neighbours():
    lat = lax.axis_index("lat")
    return place_of(lat - 1), place_of(lat + 1)


TILES = 7 * C // 8


class Chunks:
    def __init__(self, n):
        self.n = n
        self.full = 8 * TILES // n
        self.rows = self.full + 1
        self.sent = self.full + 2
        self.halves = 8 * TILES - self.full * n
        assert self.halves in (0, n // 2) and self.full * n % 8 == 0

    def pieces(self, tile):
        at, end = 8 * tile, 8 * tile + 8
        while at < end:
            now = min(self.full - at % self.full, end - at)
            yield at // self.full, at % self.full, now
            at += now


PIECES = 1


def front_kernel(x, g, own_1, own_2, west, east, x_here, g_here, sems):
    step = C // PIECES
    copies = {}
    for k in range(PIECES):
        at = pl.ds(k * step * R, step * R)
        for part, (source, here) in enumerate(((x, x_here), (g, g_here))):
            copies[k, part] = pltpu.make_async_copy(source.at[at, :], here.at[at, :], sems.at[k, part])
            copies[k, part].start()
    odd = odd_lat()
    lane = lax.broadcasted_iota(jnp.int32, (step, L), 1)
    for k in range(PIECES):
        to = pl.ds(k * step, step)
        first = jnp.zeros((step, L), F32)
        last = jnp.zeros((step, L), F32)
        for part, here in enumerate((x_here, g_here)):
            copies[k, part].wait()
            base = HALF * part
            for r in range(R):
                value = here[pl.ds(k * step * R + r, step, stride=R), :]
                if r == 0:
                    top = value
                moved = roll(value, base + r + 1)
                last = jnp.where(lane == base + r, moved, last)
                first = jnp.where(lane == base + r + 1, moved, first)
            own_1[part, to, :] = pick(odd, top, value)
            own_2[part, to, :] = pick(odd, value, top)
        west[to, :] = roll(first, -1)
        east[to, :] = roll(last, 1)


def whole_column(east, row_1, row_2):
    lane = lanes()
    column = east[...]
    odd = odd_lat()
    for part in range(2):
        north = pick(odd, row_1[part], row_2[part])
        south = pick(odd, row_2[part], row_1[part])
        column = jnp.where(lane == HALF * part, roll(north, 1 + HALF * part), column)
        column = jnp.where(lane == HALF * part + R + 1, roll(south, HALF * part + R + 2), column)
    return column


def column_kernel(east, row_1, row_2, column):
    column[...] = whole_column(east, row_1, row_2)


def taps(value, west, west_lane, east, east_lane):
    lane = lanes()
    before = jnp.where(lane == 0, roll(west, -west_lane), roll(value, 1))
    after = jnp.where(lane == L - 1, roll(east, L - 1 - east_lane), roll(value, -1))
    return before, value, after


def nt(left, right):
    return lax.dot_general(left[...], right[...], NT, preferred_element_type=F32)


def wide_form(grad, bias):
    return jnp.concatenate(
        [grad[a * C : (a + 1) * C] for a in range(3)]
        + [bias, jnp.zeros((C, 7 * L - 9 * C - bias.shape[1]), F32)],
        axis=1,
    )


def inner_taps(value):
    lane = lanes()
    before = jnp.where(lane == 0, 0.0, roll(value, 1))
    after = jnp.where(lane == L - 1, 0.0, roll(value, -1))
    return before, value, after


def inner_weight_kernel(x, g, inner, s_both, c_hi, c_lo):
    zero = jnp.zeros((C, L), F32)
    total = zero
    for a, to in ((0, R - 1), (2, 0)):
        c_hi[pl.ds(a * C, C), pl.ds(to * L, L)] = zero.astype(BF16)
        c_lo[pl.ds(a * C, C), pl.ds(to * L, L)] = zero.astype(BF16)
    for r in range(R):
        at = pl.ds(r * L, L)
        for b, shifted in enumerate(inner_taps(row(x, r))):
            s_both[pl.ds(b * C, C), at], s_both[pl.ds((3 + b) * C, C), at] = split(shifted)
        value = row(g, r)
        total = total + value
        high, low = split(value)
        for a in range(3):
            to = r + a - 1
            if 0 <= to < R:
                c_hi[pl.ds(a * C, C), pl.ds(to * L, L)] = high
                c_lo[pl.ds(a * C, C), pl.ds(to * L, L)] = low
    both = nt(c_hi, s_both)
    grad = both[:, : 3 * C] + both[:, 3 * C :] + nt(c_lo, s_both.at[pl.ds(0, 3 * C), :])
    inner[...] = wide_form(grad, jnp.sum(total, axis=1, keepdims=True))


def outer_weight_kernel(
    chunks, inner, own_east, own_1, own_2, east, row_1, row_2, packed, s_both, c_hi, c_lo
):
    lane = lanes()
    zero = jnp.zeros((C, L), F32)
    odd = odd_lat()
    north = pick(odd, row_1[1], row_2[1])
    south = pick(odd, row_2[1], row_1[1])
    x_top = pick(odd, own_1[0], own_2[0])
    x_bottom = pick(odd, own_2[0], own_1[0])
    column = whole_column(own_east, row_1, row_2)
    beyond = east[...]
    at_top = at_end(0)
    at_bottom = at_end(lax.axis_size("lat") - 1)

    def put(k, left, right):
        at = pl.ds(k * L, L)
        for part, value in enumerate(left):
            if value is None:
                c_hi[pl.ds(part * C, C), at] = c_lo[pl.ds(part * C, C), at] = jnp.zeros((C, L), BF16)
            else:
                c_hi[pl.ds(part * C, C), at], c_lo[pl.ds(part * C, C), at] = split(value)
        for part, value in enumerate(right):
            high = pl.ds(part * C, C)
            low = pl.ds((3 + part) * C, C)
            if value is None:
                s_both[high, at] = s_both[low, at] = jnp.zeros((C, L), BF16)
            else:
                s_both[high, at], s_both[low, at] = split(value)

    put(0, (north * at_top, None, north * (1.0 - at_top)), inner_taps(x_top))
    put(1, (south * (1.0 - at_bottom), None, south * at_bottom), inner_taps(x_bottom))
    g_column = roll(column, -HALF)
    below = roll(g_column, -2)
    above = g_column
    south_end = jnp.where(lane == R - 1, below * at_bottom, 0.0)
    north_end = jnp.where(lane == 0, above * at_top, 0.0)
    shifted = (below - south_end + north_end, roll(g_column, -1), above - north_end + south_end)
    left = []
    for a, value in enumerate(shifted):
        other = jnp.where(lane < HALF + a + R, roll(beyond, a), 0.0)
        left.append(jnp.where(lane < HALF, value, jnp.where(lane < HALF + a, 0.0, other)))
    own = jnp.where(lane < HALF + R + 2, roll(column, HALF), 0.0)
    put(2, left, (jnp.where(lane < HALF, 0.0, own), None, jnp.where(lane < R, beyond, 0.0)))
    both = nt(c_hi, s_both)
    grad = both[:, : 3 * C] + both[:, 3 * C :] + nt(c_lo, s_both.at[pl.ds(0, 3 * C), :])
    wide = inner[...] + wide_form(grad, jnp.zeros((C, 1), F32))
    cells = zero
    for k, at in enumerate((0, HALF, R - 1, HALF + R - 1)):
        cells = jnp.where(lane == k, roll(beyond, k - at), cells)
    cells = jnp.concatenate([cells, jnp.zeros((L - C, L), F32)], axis=0).T
    x_cells = roll(cells[0:8], HALF)
    g_cells = roll(cells[0:8], L // 4)
    lane = lax.broadcasted_iota(jnp.int32, (1, L), 1)
    corners = []
    for k in (0, 2):
        moved = x_cells[k : k + 1]
        corners.append((moved, jnp.where(lane < L // 4, moved, g_cells[k + 1 : k + 2])))
    to_north, to_south = lat_neighbours()
    left = chunks.full * chunks.n // 8
    for tile in range(TILES):
        i, j = divmod(tile, 7)
        value = wide[8 * i : 8 * i + 8, L * j : L * j + L]
        if tile < left:
            at = 0
            for chunk, place, count in chunks.pieces(tile):
                packed[pl.ds(chunk * chunks.sent + place, count), :] = value[at : at + count]
                at += count
        else:
            for k, half in enumerate((value, roll(value, HALF))):
                for r in range(8):
                    chunk = 2 * (8 * (tile - left) + r) + k
                    packed[pl.ds(chunk * chunks.sent + chunks.full, 1), :] = half[r : r + 1]
    for chunk in range(chunks.n):
        at = chunk * chunks.sent + chunks.full
        first = jnp.where(to_north == chunk, corners[0][0], jnp.where(to_south == chunk, corners[1][0], 0.0))
        if chunks.halves:
            first = jnp.where(lane < HALF, packed[pl.ds(at, 1), :], first)
        packed[pl.ds(at, 1), :] = first
        packed[pl.ds(at + 1, 1), :] = jnp.where(
            to_north == chunk, corners[0][1], jnp.where(to_south == chunk, corners[1][1], 0.0)
        )


def sum_kernel(rows, height, parts, result):
    total = parts[pl.ds(0, rows), :]
    for k in range(1, parts.shape[0] // height):
        total = total + parts[pl.ds(k * height, rows), :]
    for k in range(result.shape[0] // rows):
        result[pl.ds(k * rows, rows), :] = total


def unpack_kernel(chunks, factor, gathered, weight_grad, bias_grad):
    lane = lax.broadcasted_iota(jnp.int32, (8, L), 1)
    left = chunks.full * chunks.n // 8
    ends = []
    for tile in range(TILES):
        i, j = divmod(tile, 7)
        if tile < left:
            value = jnp.concatenate(
                [
                    gathered[pl.ds(chunk * chunks.rows + place, count), :]
                    for chunk, place, count in chunks.pieces(tile)
                ],
                axis=0,
            )
        else:
            at = 16 * (tile - left) * chunks.rows + chunks.full
            even, odd = (
                gathered[pl.ds(at + k * chunks.rows, 8, stride=2 * chunks.rows), :] for k in range(2)
            )
            value = jnp.where(lane < HALF, even, roll(odd, HALF))
        width = min(L, 9 * C - L * j)
        weight_grad[pl.ds(8 * i, 8), pl.ds(L * j, width)] = value[:, :width] * factor
        if width < L:
            ends.append(value)
    ends = jnp.concatenate(ends + [jnp.zeros((L - C, L), F32)], axis=0).T
    at = 9 * C % L
    bias_grad[...] = ends[at : at + 1, :C] * factor


def conv_kernel(
    is_grad, field, west, east, row_1, row_2, weight, bias, parts, result, token, hi, lo, ends, sems
):
    part = 1 if is_grad else 0
    copies = [
        pltpu.make_async_copy(
            parts.at[at, :, pl.ds(parts.shape[2] - 2 * L, 2 * L)], ends.at[k], sems.at[k]
        )
        for k, at in enumerate(lat_neighbours())
    ]
    for copy in copies:
        copy.start()
    odd = odd_lat()
    north = pick(odd, row_1[part], row_2[part])
    south = pick(odd, row_2[part], row_1[part])
    for copy in copies:
        copy.wait()
    lane = lax.broadcasted_iota(jnp.int32, (1, L), 1)
    corners = []
    for k in range(2):
        former, latter = ends[k][:, :L], ends[k][:, L:]
        if is_grad:
            corners.append(roll(latter, -(L // 4)))
        else:
            corners.append(jnp.where(lane < HALF, roll(former, HALF), roll(latter, HALF)))
    corners = jnp.concatenate(corners + [jnp.zeros((L - 2, L), F32)], axis=0).T[:C]
    first = HALF * part

    def shifts(r):
        if r < 0:
            return taps(north, west[...], first + r + 1, corners, 0)
        if r >= R:
            return taps(south, west[...], first + r + 1, corners, 1)
        return taps(row(field, r), west[...], first + r + 1, east[...], first + r)

    def put(block, half, values):
        for b, value in enumerate(values):
            at = (pl.ds((3 * block + b) * C, C), pl.ds(half * L, L))
            hi[at], lo[at] = split(value)

    half = R // 2
    if is_grad:
        at_top = at_end(0)
        at_bottom = at_end(lax.axis_size("lat") - 1)
        outer_top = shifts(-1)
        outer_bottom = shifts(R)
        put(0, 0, [v * (1.0 - at_top) for v in outer_top])
        put(0, 1, shifts(half - 1))
        put(1, 0, shifts(0))
        put(1, 1, shifts(half))
        put(2, 0, [v + o * at_top for v, o in zip(shifts(1), outer_top)])
        put(2, 1, shifts(half + 1))
        for r in range(half):
            put(3 + r, 0, shifts(r))
            put(3 + r, 1, shifts(r + half))
        k = 3 + half
        put(k, 0, shifts(half - 2))
        put(k, 1, [v + o * at_bottom for v, o in zip(shifts(R - 2), outer_bottom)])
        put(k + 1, 0, shifts(half - 1))
        put(k + 1, 1, shifts(R - 1))
        put(k + 2, 0, shifts(half))
        put(k + 2, 1, [v * (1.0 - at_bottom) for v in outer_bottom])
        starts = [0] + [2 + r for r in range(1, half - 1)] + [k]
    else:
        for j in range(half + 2):
            put(j, 0, shifts(j - 1))
            put(j, 1, shifts(j - 1 + half))
        starts = list(range(half))
    w_hi, w_lo = split(weight[...])
    both = jnp.concatenate([w_hi, w_lo], axis=0)
    for r, start in enumerate(starts):
        at = pl.ds(start * 3 * C, 9 * C)
        first = jnp.dot(both, hi[at, :], preferred_element_type=F32)
        second = jnp.dot(w_hi, lo[at, :], preferred_element_type=F32)
        value = first[:C] + first[C:] + second
        if not is_grad:
            value = value + bias[...]
        result[pl.ds(r, C, stride=R), :] = value[:, :L]
        result[pl.ds(r + half, C, stride=R), :] = value[:, L:]
    token[...] = jnp.zeros((8, L), F32)


def flip_kernel(weight, flipped):
    blocks = []
    for tap in reversed(range(9)):
        block = jnp.concatenate([weight[:, tap * C : (tap + 1) * C], jnp.zeros((C, L - C), F32)], axis=1)
        block = jnp.concatenate([block, jnp.zeros((L - C, L), F32)], axis=0)
        blocks.append(block.T[:C, :C])
    flipped[...] = jnp.concatenate(blocks, axis=1)


def conv(is_grad, *args, after=()):
    blocks = 3 + R // 2 + 3 if is_grad else R // 2 + 2
    scratch = pltpu.VMEM((blocks * 3 * C, 2 * L), BF16)
    return call(
        functools.partial(conv_kernel, is_grad),
        [out(C * R, L), out(8, L)],
        args,
        [scratch, scratch, pltpu.VMEM((2, 1, 2 * L), F32), pltpu.SemaphoreType.DMA((2,))],
        after,
        specs=[VMEM] * (len(args) - 1) + [ANY],
        flops=4 * 6 * 9 * C * C * R * L,
        moved=3 * 4 * C * R * L,
    )


def shards(nlat, nlon, factor, x, weight, bias, g):
    x = x.reshape(C * R, L)
    g = g.reshape(C * R, L)

    def pairs_of(partner):
        pairs = []
        for i in range(nlat):
            for j in range(nlon):
                to_lat, to_lon = partner(i, j)
                pairs.append((i * nlon + j, to_lat * nlon + to_lon))
        return pairs

    def across_2(i, j):
        to = i + 1 if i % 2 else i - 1
        return (to, j) if 0 <= to < nlat else (i, (j + nlon // 2) % nlon)

    to_west = pairs_of(lambda i, j: (i, (j - 1) % nlon))
    to_east = pairs_of(lambda i, j: (i, (j + 1) % nlon))
    first = pairs_of(lambda i, j: (i ^ 1, j))
    second = pairs_of(across_2)

    def send(value, pairs):
        return lax.ppermute(value, AXES, pairs)

    block = 4 * C * R * L
    product = 6 * 9 * C * C * R * L
    own_1, own_2, own_west, own_east, x, g = call(
        front_kernel,
        [kept(2, C, L)] * 2 + [kept(C, L)] * 2 + [kept(C * R, L)] * 2,
        (in_hbm(x), in_hbm(g)),
        [pltpu.SemaphoreType.DMA((PIECES, 2))],
        specs=[ANY] * 2,
        flops=block,
        moved=2 * block,
    )
    row_2 = send(own_2, second)
    row_1 = send(own_1, first)
    east = send(own_west, to_west)
    inner = call(
        inner_weight_kernel,
        [out(C, 7 * L)],
        (x, g),
        [pltpu.VMEM((6 * C, R * L), BF16)] + [pltpu.VMEM((3 * C, R * L), BF16)] * 2,
        flops=product,
        moved=2 * block,
    )[0]

    n_far = lax.axis_size(FAR)
    n_near = nlat * nlon // n_far
    chunks = Chunks(n_near)
    packed = call(
        functools.partial(outer_weight_kernel, chunks),
        [out(n_near * chunks.sent, L)],
        (inner, own_east, own_1, own_2, east, row_1, row_2),
        [pltpu.VMEM((6 * C, 3 * L), BF16)] + [pltpu.VMEM((3 * C, 3 * L), BF16)] * 2,
        flops=product // 4,
        moved=block,
    )[0]
    parts = lax.all_to_all(packed.reshape(n_near, 1, chunks.sent * L), NEAR, 0, 0)
    mine = call(
        functools.partial(sum_kernel, chunks.rows, chunks.sent),
        [out(n_far * chunks.rows, L)],
        (parts.reshape(n_near * chunks.sent, L),),
        moved=block // 2,
    )[0]
    column = call(column_kernel, [kept(C, L)], (own_east, row_1, row_2), after=(mine,))[0]
    west = send(column, to_east)
    others = lax.all_to_all(mine.reshape(n_far, 1, chunks.rows * L), FAR, 0, 0)
    flipped = call(flip_kernel, [kept(C, 9 * C)], (weight,), after=(column,))[0]
    halo = (west, east, row_1, row_2)
    bias = bias.reshape(C, 1)
    mine = call(
        functools.partial(sum_kernel, chunks.rows, chunks.rows),
        [out(n_near * chunks.rows, L)],
        (others.reshape(n_far * chunks.rows, L),),
        after=(west, flipped, bias),
        moved=block // 2,
    )[0]
    gathered = lax.all_to_all(mine.reshape(n_near, 1, chunks.rows * L), NEAR, 0, 0)
    output, _ = conv(False, x, *halo, weight, bias, parts, after=(mine,))
    grad, _ = conv(True, g, *halo, flipped, bias, parts, after=(mine,))
    weight_grad, bias_grad = call(
        functools.partial(unpack_kernel, chunks, factor),
        [out(C, 9 * C), out(1, C)],
        (gathered.reshape(n_near * chunks.rows, L),),
        moved=block,
    )
    return (
        output.reshape(C, R, L),
        grad.reshape(C, R, L),
        weight_grad,
        bias_grad.reshape(C),
    )


def solution(mesh):
    nlat, nlon = mesh.shape["lat"], mesh.shape["lon"]
    fine = Mesh(mesh.devices.reshape(nlat, 2, nlon // 8, 2, 2), AXES)
    factor = 1.0 / math.sqrt(nlat * R * nlon * L)
    field = P(None, "lat", LON)
    return jax.shard_map(
        functools.partial(shards, nlat, nlon, factor),
        mesh=fine,
        in_specs=(field, P(), P(), field),
        out_specs=(field, field, P(), P()),
        check_vma=False,
    )
```
